128 devices in a mesh: gx: 4 (over z), gy: 4 (over y), gz: 8 (over x, core).
Axes of the slice: x: 4, y: 4, z: 4, core: 2. Of those that a mesh axis runs over, the one named last changes fastest.
Arguments:
- old_state: float32 [16, 32, 64, 1024], P(None, 'gx', 'gy', 'gz'), may hold values from -12 to 12
- remap_weights: bfloat16 [16384, 4, 128, 128], P(('gx', 'gy', 'gz')), may hold values from -0.176776695 to 0.609375
- new_owner: int32 [16384, 1], P(('gx', 'gy', 'gz')), may hold values from 0 to 127; in each aligned block of 128 rows (0 to 127, 128 to 255, ...) at most 2 rows name the same one
- new_block: int32 [16384], P(('gx', 'gy', 'gz')), may hold values from 0 to 127
Outputs:
- new_state: float32 [16, 32, 64, 1024], P(None, 'gx', 'gy', 'gz')
The draws below stay inside these ranges and needn't reach their ends.
Inputs may be any that keep to these rules, and one draw needn't show every extreme that they name: `new_owner`: A device is numbered in mesh order, gx slowest and gz fastest. The 128 rows of one device name any one device at most 2 times.
All inputs are finite; a program needn't handle non-finite values.
Results may differ from the reference program's by a relative error of at most 0.0003.
The reference program's roundings to bfloat16 on the way (of `moments`) count: a program that leaves them out, or rounds other values in their place, can miss the bound.
Values sent between devices are 32-bit elements; how exact they have to be, the bound alone decides.
A program may use at most 64 MiB of HBM per device.

```python
import math
import jax
import jax.numpy as jnp
import numpy as np
from jax import lax

FIELDS = 16
CX = 8
CY = 16
CZ = 128
OB = 128
OLD_BLOCKS = 16384
CAP = 2
NX = 32
NY = 64
NZ = 1024
N_GX = 4
N_GY = 4
N_GZ = 8
DEVICES = 128


def draw_old_state(key, part):
    key = jax.random.fold_in(key, 11)
    first_key = jax.random.fold_in(key, 0)
    full_shape = (FIELDS, NX, NY, NZ)
    amplitude = (1.0 + 2.0 * jnp.arange(NX, dtype=jnp.float32) / max(NX - 1, 1)).reshape(1, NX, 1, 1)
    values = jnp.clip(jax.random.normal(first_key, full_shape, jnp.float32), -4.0, 4.0) * amplitude
    return values.astype(jnp.float32)


def draw_remap_weights(key, part):
    key = jax.random.fold_in(key, 23)
    identity_mask = (jnp.arange(CZ)[:, None] == jnp.arange(CZ)[None, :]).astype(jnp.float32)

    def one_device(device_key):
        volume_key, moment_key = jax.random.split(device_key)
        volume_part = jax.random.uniform(volume_key, (OB, 1, CZ, CZ), jnp.float32, 0.0, 0.8 / CZ)
        moment_part = jnp.clip(jax.random.normal(moment_key, (OB, 3, CZ, CZ), jnp.float32), -4.0, 4.0) * (0.5 / math.sqrt(CZ))
        return jnp.concatenate([0.6 * identity_mask + volume_part, moment_part], axis=1).astype(jnp.bfloat16)
    device_keys = jax.random.split(key, DEVICES)
    return lax.map(one_device, device_keys).reshape(OLD_BLOCKS, 4, CZ, CZ)


def place_ends(array, rng, smallest, high):
    shape = array.shape
    index_at = [jax.random.randint(jax.random.fold_in(rng, axis), (), 0, shape[axis]) for axis in range(len(shape))]
    array = array.at[tuple(index_at)].set(smallest)
    longest = shape.index(max(shape))
    index_at[longest] = (index_at[longest] + 1) % shape[longest]
    return array.at[tuple(index_at)].set(high)


def deal_out(rng, own, number, rows, count, top, bound, lean):
    sequence = jax.random.permutation(rng, count)
    heavy_load, common = portions_of(count, rows * top, bound, lean, True), portions_of(count, rows * top, bound, lean, False)
    places = jnp.arange(count)

    def named(tallies, rotation):
        used = int((tallies > 0).sum())
        fixed = max(1, used // 4)
        moved = fixed + (places - fixed + rotation * (used - fixed)) % max(1, count - fixed)
        return jnp.zeros((count,), jnp.int32).at[sequence[jnp.where(places < fixed, places, moved)]].set(jnp.asarray(tallies, jnp.int32))

    tallies = jnp.where(number % 4 == 0, named(heavy_load, number // 4), named(common, number - number // 4 - 1))
    mixed = jax.random.permutation(jax.random.fold_in(own, 3), count)
    giver, receiver = mixed[0:count // 2 * 2:2], mixed[1:count // 2 * 2:2]
    margin = jnp.minimum(tallies[giver] - 1, bound - tallies[receiver]) // 2
    margin = jnp.where((giver == sequence[0]) | (receiver == sequence[0]) | (tallies[receiver] == 0), 0, jnp.maximum(margin, 0))
    moved = jax.random.randint(jax.random.fold_in(own, 4), (count // 2,), 0, 1 << 20) % (margin + 1)
    tallies = tallies.at[giver].add(-moved).at[receiver].add(moved)
    items = jnp.searchsorted(jnp.cumsum(tallies), jnp.arange(rows * top), side="right").astype(jnp.int32)
    table = items.reshape(top, rows).T
    table = table[jax.random.permutation(jax.random.fold_in(own, 1), rows)]
    rotation = jax.random.randint(jax.random.fold_in(own, 2), (rows, 1), 0, top)
    return jnp.take_along_axis(table, (jnp.arange(top)[None, :] + rotation) % top, axis=1)


def portions_of(count, total, bound, skew, full):
    portions = [(1 << 20) // math.isqrt(standing ** skew) + 1 for standing in range(1, count + 1)]
    largest = bound if full else min(bound, max(-(-total // count), total * portions[0] // sum(portions)))
    least = 1 if total - largest >= count - 1 else 0
    holding, spare = [largest] + [least] * (count - 1), total - largest - least * (count - 1)
    while spare > 0:
        free = [i for i in range(1, count) if holding[i] < largest] or [i for i in range(1, count) if holding[i] < bound]
        pool, left = sum([portions[i] for i in free]), spare
        for i in free:
            extra = min(bound - holding[i], max(1, left * portions[i] // pool), spare)
            holding[i] = holding[i] + extra
            spare = spare - extra
    return np.array(holding)


def setup_inputs(seed: int = 0) -> dict:
    key_list = jax.random.split(jax.random.key(seed), 5)
    old_state = draw_old_state(jax.random.fold_in(key_list[4], 71), 0)
    remap_weights = draw_remap_weights(jax.random.fold_in(key_list[4], 71), 0)
    new_owner_keys = jax.random.split(jax.random.fold_in(key_list[2], 1), OLD_BLOCKS // OB)
    new_owner_turns = jax.random.permutation(jax.random.fold_in(key_list[2], 3), OLD_BLOCKS // OB)
    new_owner = jax.vmap(lambda own, number: deal_out(jax.random.fold_in(key_list[2], 2), own, number, OB, DEVICES, 1, CAP, 2))(new_owner_keys, new_owner_turns).reshape((OLD_BLOCKS, 1))
    new_block = place_ends(jax.random.randint(key_list[3], (OLD_BLOCKS,), 0, OB), jax.random.fold_in(key_list[3], 1), 0, OB - 1).astype(jnp.int32)
    return dict(old_state=old_state, remap_weights=remap_weights, new_owner=new_owner, new_block=new_block)


def shifted(values, dimension, low_cut, high_cut):
    return lax.slice_in_dim(values, low_cut, values.shape[dimension] - high_cut, axis=dimension)

def trimmed(values, dimensions):
    for dimension in dimensions:
        values = shifted(values, dimension, 1, 1)
    return values

def limited(padded):
    center = trimmed(padded, (1, 2, 3))
    slopes = []
    for dimension in (1, 2, 3):
        remaining = tuple((entry for entry in (1, 2, 3) if entry != dimension))
        strip_cells = trimmed(padded, remaining)
        below_step = center - shifted(strip_cells, dimension, 0, 2)
        above_step = shifted(strip_cells, dimension, 2, 0) - center
        slopes.append(0.5 * (jnp.sign(below_step) + jnp.sign(above_step)) * jnp.minimum(jnp.abs(below_step), jnp.abs(above_step)))
    return jnp.stack([center] + slopes)

def smooth(values, dimension):
    return shifted(values, dimension, 0, 2) + 2.0 * shifted(values, dimension, 1, 1) + shifted(values, dimension, 2, 0)

def spread(values, dimension):
    return shifted(values, dimension, 2, 0) - shifted(values, dimension, 0, 2)

def wave_speed(fields):
    velocity_sq = fields[1] * fields[1] + fields[2] * fields[2] + fields[3] * fields[3]
    return jnp.sqrt(1.0 + 0.05 * (fields[4] * fields[4] + velocity_sq))

def lagrange_step(fields, padded_rim, speed_max):
    pressure = padded_rim[0]
    grad_x = spread(smooth(smooth(pressure, 1), 2), 0) / 32.0
    grad_y = spread(smooth(smooth(pressure, 0), 2), 1) / 32.0
    grad_z = spread(smooth(smooth(pressure, 0), 1), 2) / 32.0
    divergence = (spread(smooth(smooth(padded_rim[1], 1), 2), 0) + spread(smooth(smooth(padded_rim[2], 0), 2), 1) + spread(smooth(smooth(padded_rim[3], 0), 1), 2)) / 32.0
    time_step = 0.5 / speed_max
    new_pressure = fields[0] - time_step * divergence
    new_velocity = fields[1:4] - time_step * jnp.stack([grad_x, grad_y, grad_z])
    new_energy = fields[4] - time_step * fields[0] * divergence
    return jnp.concatenate([new_pressure[None], new_velocity, new_energy[None], fields[5:]], axis=0)

def contribute(pair):
    return jnp.einsum('bkfi,bkij->bfj', pair[0].astype(jnp.float32), pair[1].astype(jnp.float32), precision=lax.Precision.HIGHEST)

def reference(old_state, remap_weights, new_owner, new_block):
    padded = jnp.pad(old_state, ((0, 0), (1, 1), (1, 1), (1, 1)))
    moments = limited(padded).astype(jnp.bfloat16)
    moments = moments.reshape(4, FIELDS, N_GX, CX, N_GY, CY, N_GZ, CZ).transpose(2, 4, 6, 3, 5, 0, 1, 7)
    moments = moments.reshape(DEVICES, OB, 4, FIELDS, CZ)
    weights = remap_weights.reshape(DEVICES, OB, 4, CZ, CZ)
    contributions = lax.map(contribute, (moments, weights)).reshape(OLD_BLOCKS, FIELDS, CZ)
    targets = (new_owner[:, 0].astype(jnp.int32) * OB + new_block.astype(jnp.int32)).astype(jnp.int32)
    blocks = jnp.zeros((OLD_BLOCKS, FIELDS, CZ), jnp.float32).at[targets].add(contributions)
    fields = blocks.reshape(N_GX, N_GY, N_GZ, CX, CY, FIELDS, CZ).transpose(5, 0, 3, 1, 4, 2, 6).reshape(FIELDS, NX, NY, NZ)
    padded_rim = jnp.pad(fields[0:4], ((0, 0), (1, 1), (1, 1), (1, 1)))
    speed_max = jnp.max(wave_speed(fields))
    return lagrange_step(fields, padded_rim, speed_max)
```

```python
import jax
import jax.numpy as jnp
from jax import lax
from jax.experimental import pallas as pl
from jax.experimental.pallas import tpu as pltpu
from jax.sharding import PartitionSpec as P

MESH = pl.DeviceIdType.MESH
F32 = jnp.float32
BF16 = jnp.bfloat16
CHUNKS = 4
STEPS = 128 // CHUNKS


def four(j):
    return (2 + j * (j + 1) // 2) % 4


def eight(j):
    return (4 + ((j + 1) // 2) * (2 * (j % 2) - 1) + 8) % 8


def offsets(i):
    return four(i % 4), four((i // 4 + i + 1) % 4), eight((i // 16 + i // 4 + i + 2) % 8)


def limit(below, above):
    return jnp.maximum(jnp.minimum(below, above), 0.0) + jnp.minimum(jnp.maximum(below, above), 0.0)


def kernel(
    state, weights, owner, block, out,
    w, nat, pad, zsend, zrecv, contrib, sendbuf, recvbuf, meta, metat, slotv, slots, lhs, rhs, fields, rim,
    xrecv, ysend, yrecv, erecv, zcol, zcolr, max1, max2,
    w_sem, in_sem, slot_sem, out_sem, halo_s, halo_r, m1_s, m1_r, m2_s, m2_r, a2a_s, a2a_r, rim_s, rim_r,
    x1_s, x1_r, x2_s, x2_r,
):
    gx, gy, gz = lax.axis_index("gx"), lax.axis_index("gy"), lax.axis_index("gz")
    plane = gx * 4 + gy
    me = plane * 8 + gz

    def at(a, b, c):
        return ((gx + a + 4) % 4, (gy + b + 4) % 4, (gz + c + 8) % 8)

    def remote(src, dst, send, recv, device):
        return pltpu.make_async_remote_copy(
            src_ref=src, dst_ref=dst, send_sem=send, recv_sem=recv, device_id=device, device_id_type=MESH
        )

    load_state = pltpu.make_async_copy(state, nat, in_sem.at[0])
    load_state.start()

    def load_weights(x):
        return pltpu.make_async_copy(weights.at[pl.ds(x * 16, 16)], w.at[pl.ds(x * 16, 16)], w_sem.at[x])

    for x in (1, 2, 3, 4, 5, 6, 0, 7):
        load_weights(x).start()
    barrier = pltpu.get_barrier_semaphore()

    def greet(t, carry):
        pl.semaphore_signal(
            barrier, inc=1, device_id=((gx + t // 32) % 4, (gy + (t // 8) % 4) % 4, (gz + t % 8) % 8),
            device_id_type=MESH,
        )
        return carry

    lax.fori_loop(1, 128, greet, 0)

    lane = lax.broadcasted_iota(jnp.int32, (128, 128), 1)
    sub = lax.broadcasted_iota(jnp.int32, (128, 128), 0)
    named = jnp.broadcast_to(owner[...], (128, 128)).T == lane
    first = jnp.min(jnp.where(named, sub, 128), axis=0, keepdims=True)
    last = jnp.max(jnp.where(named, sub, -1), axis=0, keepdims=True)
    slotv[...] = jnp.concatenate([first, jnp.where(last > first, last, 128)] * 4, axis=0)
    fetch_slots = pltpu.make_async_copy(slotv, slots, slot_sem.at[0])
    fetch_slots.start()
    meta[plane, gz] = jnp.concatenate([owner[...], block[...]], axis=0)
    contrib[128] = jnp.zeros((16, 128), F32)

    load_state.wait()
    lane16 = lax.broadcasted_iota(jnp.int32, (16, 128), 1)

    def to_blocks(x, carry):
        low, high = carry
        for part in range(2):
            for half in range(2):
                tile = nat[pl.ds(half * 8, 8), x, pl.ds(part * 8, 8), :]
                pad[x + 1, pl.ds(1 + part * 8, 8), pl.ds(half * 8, 8), :] = jnp.swapaxes(tile, 0, 1)
        for y in range(16):
            b = x * 16 + y
            rolled = pltpu.roll(pad[x + 1, y + 1], b, 1)
            low = jnp.where(lane16 == b, rolled, low)
            high = jnp.where(lane16 == (b + 127) % 128, rolled, high)
        return low, high

    zeros = jnp.zeros((16, 128), F32)
    low, high = lax.fori_loop(0, 8, to_blocks, (zeros, zeros))
    zsend[0] = low
    zsend[1] = pltpu.roll(high, 1, 1)
    pl.semaphore_wait(barrier, 127)

    z_up = remote(zsend.at[1], zrecv.at[0], halo_s.at[0], halo_r.at[0], at(0, 0, 1))
    z_down = remote(zsend.at[0], zrecv.at[1], halo_s.at[1], halo_r.at[1], at(0, 0, -1))
    inner = pl.ds(1, 16)
    cells = pl.ds(1, 8)
    x_up = remote(pad.at[8, inner], pad.at[0, inner], halo_s.at[2], halo_r.at[2], at(1, 0, 0))
    x_down = remote(pad.at[1, inner], pad.at[9, inner], halo_s.at[3], halo_r.at[3], at(-1, 0, 0))
    y_up = remote(pad.at[cells, 16], pad.at[cells, 0], halo_s.at[4], halo_r.at[4], at(0, 1, 0))
    y_down = remote(pad.at[cells, 1], pad.at[cells, 17], halo_s.at[5], halo_r.at[5], at(0, -1, 0))
    for copy in (z_up, z_down, x_up, x_down, y_up, y_down):
        copy.start()

    def meta_one(c):
        mine = meta.at[plane, gz]
        return remote(mine, mine, m1_s.at[c], m1_r.at[c], (gx, gy, (gz + c) % 8))

    def meta_two(e):
        to = (plane + e) % 16
        return remote(meta.at[plane], meta.at[plane], m2_s.at[e], m2_r.at[e], (to // 4, to % 4, gz))

    def start_all(make, lo, hi):
        def body(i, carry):
            make(i).start()
            return carry
        lax.fori_loop(lo, hi, body, 0)

    def recv_all(make, lo, hi):
        def body(i, carry):
            make(i).wait_recv()
            return carry
        lax.fori_loop(lo, hi, body, 0)

    def sent_all(make, lo, hi):
        def body(i, carry):
            make(i).wait_send()
            return carry
        lax.fori_loop(lo, hi, body, 0)

    start_all(meta_one, 1, 8)

    z_up.wait_recv()
    z_down.wait_recv()
    z_low = jnp.where(gz == 0, 0.0, zrecv[0])
    z_high = jnp.where(gz == 7, 0.0, zrecv[1])

    def contribute(x, y):
        b = (x - 1) * 16 + (y - 1)
        q = pad[x, y]
        before = jnp.where(lane16 == 0, pltpu.roll(z_low, (128 - b) % 128, 1), pltpu.roll(q, 1, 1))
        after = jnp.where(lane16 == 127, pltpu.roll(z_high, 127 - b, 1), pltpu.roll(q, 127, 1))
        moments = jnp.concatenate(
            [
                q,
                limit(q - pad[x - 1, y], pad[x + 1, y] - q),
                limit(q - pad[x, y - 1], pad[x, y + 1] - q),
                limit(q - before, after - q),
            ],
            axis=1,
        ).astype(BF16)
        contrib[b] = jnp.dot(moments, w[b], preferred_element_type=F32)

    def inner_plane(x, carry):
        load_weights(x - 1).wait()
        for y in range(2, 16):
            contribute(x, y)
        return carry

    lax.fori_loop(2, 8, inner_plane, 0)
    recv_all(meta_one, 1, 8)
    start_all(meta_two, 1, 16)
    for copy in (x_up, x_down, y_up, y_down):
        copy.wait_recv()

    @pl.when(gx == 0)
    def _():
        pad[0, 1:17] = jnp.zeros((16, 16, 128), F32)

    @pl.when(gx == 3)
    def _():
        pad[9, 1:17] = jnp.zeros((16, 16, 128), F32)

    @pl.when(gy == 0)
    def _():
        pad[1:9, 0] = jnp.zeros((8, 16, 128), F32)

    @pl.when(gy == 3)
    def _():
        pad[1:9, 17] = jnp.zeros((8, 16, 128), F32)

    def side_columns(x, carry):
        contribute(x, 1)
        contribute(x, 16)
        return carry

    lax.fori_loop(2, 8, side_columns, 0)
    load_weights(0).wait()
    load_weights(7).wait()

    def side_planes(side, carry):
        for y in range(1, 17):
            contribute(1 + side * 7, y)
        return carry

    lax.fori_loop(0, 2, side_planes, 0)
    fetch_slots.wait()

    def delivery(i):
        a, b, c = offsets(i)
        return remote(sendbuf.at[i], recvbuf.at[i], a2a_s.at[i], a2a_r.at[i], at(a, b, c))

    def deliver(i, carry):
        a, b, c = offsets(i)
        x, y, z = at(a, b, c)
        to = x * 32 + y * 8 + z
        for slot in range(2):
            sendbuf[i, slot] = contrib[jnp.clip(slots[slot, to], 0, 128)]
        delivery(i).start()
        return carry

    lax.fori_loop(0, 127, deliver, 0)
    for slot in range(2):
        recvbuf[127, slot] = contrib[jnp.clip(slots[slot, me], 0, 128)]

    recv_all(meta_two, 1, 16)

    def in_order(i, carry):
        a, b, c = offsets(i)
        x, y, z = at(-a, -b, -c)
        row = meta[x * 4 + y, z]
        metat[0, pl.ds(i, 1), :] = row[0:1]
        metat[1, pl.ds(i, 1), :] = row[1:2]
        return carry

    lax.fori_loop(0, 128, in_order, 0)
    mine = metat[0] == me
    target = metat[1].astype(F32)
    lane = lane.astype(F32)
    first = jnp.min(jnp.where(mine, lane, 128.0), axis=1, keepdims=True)
    last = jnp.max(jnp.where(mine, lane, -1.0), axis=1, keepdims=True)
    target_0 = jnp.max(jnp.where(mine & (lane == first), target, -1.0), axis=1, keepdims=True)
    target_1 = jnp.max(jnp.where(mine & (lane == last) & (last > first), target, -1.0), axis=1, keepdims=True)
    hot_0 = jnp.where(target_0 == lane, 1.0, 0.0)
    hot_1 = jnp.where(target_1 == lane, 1.0, 0.0)
    for chunk in range(CHUNKS):
        rows = slice(chunk * STEPS, (chunk + 1) * STEPS)
        both = jnp.concatenate([hot_0[rows], hot_1[rows], hot_0[rows], hot_1[rows]], axis=0)
        lhs[chunk] = both.T.astype(BF16)

    for chunk in range(CHUNKS):
        recv_all(delivery, chunk * STEPS, min((chunk + 1) * STEPS, 127))
        for part in range(STEPS // 16):
            for slot in range(2):
                for half in range(2):
                    tile = recvbuf[pl.ds(chunk * STEPS + part * 16, 16), slot, pl.ds(half * 8, 8), :]
                    tile = jnp.swapaxes(tile, 0, 1)
                    upper = tile.astype(BF16)
                    lower = (tile - upper.astype(F32)).astype(BF16)
                    row = slot * STEPS + part * 16
                    rhs[pl.ds(half * 8, 8), pl.ds(row, 16), :] = upper
                    rhs[pl.ds(half * 8, 8), pl.ds(2 * STEPS + row, 16), :] = lower

        def accumulate(f, carry):
            part_sum = jnp.dot(lhs[chunk], rhs[f], preferred_element_type=F32)
            fields[f] = part_sum if chunk == 0 else fields[f] + part_sum
            return carry

        lax.fori_loop(0, 16, accumulate, 0)

    square = fields[4] * fields[4] + (fields[1] * fields[1] + fields[2] * fields[2] + fields[3] * fields[3])
    max1[gz] = jnp.max(square.reshape(16, 8, 128), axis=0)

    def speed_one(c):
        mine = max1.at[gz]
        return remote(mine, mine, x1_s.at[c], x1_r.at[c], (gx, gy, (gz + c) % 8))

    def speed_two(e):
        to = (plane + e) % 16
        return remote(max2.at[plane], max2.at[plane], x2_s.at[e], x2_r.at[e], (to // 4, to % 4, gz))

    start_all(speed_one, 1, 8)
    store_rest = pltpu.make_async_copy(fields.at[pl.ds(5, 11)], out.at[pl.ds(5, 11)], out_sem.at[0])
    store_rest.start()

    rim_copies = []

    def rim_send(src, dst, device):
        k = len(rim_copies)
        copy = remote(src, dst, rim_s.at[k], rim_r.at[k], device)
        copy.start()
        rim_copies.append(copy)

    rim_send(fields.at[pl.ds(0, 4), pl.ds(112, 16)], xrecv.at[0], at(1, 0, 0))
    rim_send(fields.at[pl.ds(0, 4), pl.ds(0, 16)], xrecv.at[1], at(-1, 0, 0))
    for f in range(4):
        planes = fields[f].reshape(8, 16, 128)
        ysend[0, f] = planes[:, 0]
        ysend[1, f] = planes[:, 15]
    rim_send(ysend.at[1], yrecv.at[0], at(0, 1, 0))
    rim_send(ysend.at[0], yrecv.at[1], at(0, -1, 0))
    for dx in (1, -1):
        for dy in (1, -1):
            rim_send(ysend.at[(1 + dy) // 2], erecv.at[(1 - dx) // 2, (1 - dy) // 2], at(dx, dy, 0))

    def columns(x, carry):
        low, high = carry
        for f in range(4):
            l = (x + 1) * 4 + f
            rolled = pltpu.roll(fields[f, pl.ds(pl.multiple_of(x * 16, 16), 16), :], l, 1)
            low = jnp.where(lane16 == l, rolled, low)
            high = jnp.where(lane16 == l - 1, rolled, high)
        return low, high

    low, high = lax.fori_loop(0, 8, columns, (zeros, zeros))
    zcol[0] = low
    zcol[1] = pltpu.roll(high, 1, 1)
    for dx in (0, 1, -1):
        for dy in (0, 1, -1):
            rim_send(zcol.at[1], zcolr.at[0, 1 - dx, 1 - dy], at(dx, dy, 1))
            rim_send(zcol.at[0], zcolr.at[1, 1 - dx, 1 - dy], at(dx, dy, -1))

    recv_all(speed_one, 1, 8)
    max2[plane] = jnp.max(max1[...], axis=0)
    start_all(speed_two, 1, 16)

    for copy in rim_copies:
        copy.wait_recv()
    sub8 = lax.broadcasted_iota(jnp.int32, (8, 128), 0)
    no_xl, no_xh = gx == 0, gx == 3
    no_yl, no_yh = gy == 0, gy == 3

    def tail(above, below):
        above = jnp.where(no_yh, 0.0, above)
        below = jnp.where(no_yl, 0.0, below)
        return jnp.where(sub8 == 7, below, above)

    for f in range(4):
        for x in range(8):
            rim[f, x + 1, 0:16] = fields[f, x * 16 : x * 16 + 16]
            rim[f, x + 1, 16:24] = tail(
                jnp.broadcast_to(yrecv[1, f, x : x + 1], (8, 128)), jnp.broadcast_to(yrecv[0, f, x : x + 1], (8, 128))
            )
        for side, x, none, edge in ((0, 0, no_xl, 7), (1, 9, no_xh, 0)):
            rim[f, x, 0:16] = jnp.where(none, 0.0, xrecv[side, f])
            rim[f, x, 16:24] = jnp.where(
                none,
                0.0,
                tail(
                    jnp.broadcast_to(erecv[side, 1, f, edge : edge + 1], (8, 128)),
                    jnp.broadcast_to(erecv[side, 0, f, edge : edge + 1], (8, 128)),
                ),
            )

    lane24 = lax.broadcasted_iota(jnp.int32, (24, 128), 1)

    def gathered(side, none):
        tiles = []
        for dx in range(3):
            tiles.append(
                jnp.concatenate(
                    [zcolr[side, dx, 1], tail(zcolr[side, dx, 2, 0:8], zcolr[side, dx, 0, 8:16])], axis=0
                )
            )
        below = jnp.where(no_xl, 0.0, pltpu.roll(tiles[0], 96, 1))
        above = jnp.where(no_xh, 0.0, pltpu.roll(tiles[2], 32, 1))
        whole = jnp.where(lane24 < 4, below, jnp.where(lane24 < 36, tiles[1], above))
        return jnp.where(none, 0.0, whole)

    z_low = gathered(0, gz == 0)
    z_high = gathered(1, gz == 7)

    def along_z(f, x):
        q = rim[f, x]
        l = x * 4 + f
        before = jnp.where(lane24 == 0, pltpu.roll(z_low, (128 - l) % 128, 1), pltpu.roll(q, 1, 1))
        after = jnp.where(lane24 == 127, pltpu.roll(z_high, 127 - l, 1), pltpu.roll(q, 127, 1))
        return before + 2.0 * q + after, after - before

    def smooth_y(v):
        return (pltpu.roll(v, 1, 0) + 2.0 * v + pltpu.roll(v, 23, 0))[0:16]

    def spread_y(v):
        return (pltpu.roll(v, 23, 0) - pltpu.roll(v, 1, 0))[0:16]

    def plane_terms(x):
        p_s, p_d = along_z(0, x)
        u_s, _ = along_z(1, x)
        v_s, _ = along_z(2, x)
        _, w_d = along_z(3, x)
        return (
            smooth_y(p_s), spread_y(p_s), smooth_y(p_d),
            smooth_y(u_s), spread_y(v_s) + smooth_y(w_d),
        )

    def differences(x, carry):
        before, here = carry
        after = plane_terms(x + 1)
        gradient = (
            after[0] - before[0],
            before[1] + 2.0 * here[1] + after[1],
            before[2] + 2.0 * here[2] + after[2],
        )
        divergence = after[3] - before[3] + (before[4] + 2.0 * here[4] + after[4])
        rim[3, x - 1, 0:16] = divergence * (1.0 / 32.0)
        for k in range(3):
            rim[k, x - 1, 0:16] = gradient[k] * (1.0 / 32.0)
        return here, after

    lax.fori_loop(1, 9, differences, (plane_terms(0), plane_terms(1)))
    recv_all(speed_two, 1, 16)
    largest = jnp.max(jnp.max(max2[...], axis=0), axis=(0, 1), keepdims=True)
    step = 0.5 / jnp.sqrt(1.0 + 0.05 * largest)
    step = jnp.broadcast_to(step, (16, 128))

    def advance(x, carry):
        rows = pl.ds(pl.multiple_of(x * 16, 16), 16)
        divergence = rim[3, x, 0:16]
        pressure = fields[0, rows]
        fields[4, rows] = fields[4, rows] - step * pressure * divergence
        fields[0, rows] = pressure - step * divergence
        for k in range(3):
            fields[1 + k, rows] = fields[1 + k, rows] - step * rim[k, x, 0:16]
        return carry

    for copy in rim_copies:
        copy.wait_send()
    lax.fori_loop(0, 8, advance, 0)
    store = pltpu.make_async_copy(fields.at[pl.ds(0, 5)], out.at[pl.ds(0, 5)], out_sem.at[1])
    store.start()
    for copy in (z_up, z_down, x_up, x_down, y_up, y_down):
        copy.wait_send()
    sent_all(meta_one, 1, 8)
    sent_all(meta_two, 1, 16)
    sent_all(delivery, 0, 127)
    sent_all(speed_one, 1, 8)
    sent_all(speed_two, 1, 16)
    store_rest.wait()
    store.wait()


def on_device(old_state, remap_weights, new_owner, new_block):
    dma = pltpu.SemaphoreType.DMA
    any_space = pl.BlockSpec(memory_space=pl.ANY)
    vmem = pl.BlockSpec(memory_space=pltpu.VMEM)
    out = pl.pallas_call(
        kernel,
        out_shape=jax.ShapeDtypeStruct((16, 128, 128), F32),
        in_specs=[any_space, any_space, vmem, vmem],
        out_specs=any_space,
        scratch_shapes=[
            pltpu.VMEM((128, 512, 128), BF16),
            pltpu.VMEM((16, 8, 16, 128), F32),
            pltpu.VMEM((10, 18, 16, 128), F32),
            pltpu.VMEM((2, 16, 128), F32),
            pltpu.VMEM((2, 16, 128), F32),
            pltpu.VMEM((129, 16, 128), F32),
            pltpu.VMEM((128, 2, 16, 128), F32),
            pltpu.VMEM((128, 2, 16, 128), F32),
            pltpu.VMEM((16, 8, 2, 128), jnp.int32),
            pltpu.VMEM((2, 128, 128), jnp.int32),
            pltpu.VMEM((8, 128), jnp.int32),
            pltpu.SMEM((8, 128), jnp.int32),
            pltpu.VMEM((CHUNKS, 128, 128), BF16),
            pltpu.VMEM((16, 128, 128), BF16),
            pltpu.VMEM((16, 128, 128), F32),
            pltpu.VMEM((4, 10, 24, 128), F32),
            pltpu.VMEM((2, 4, 16, 128), F32),
            pltpu.VMEM((2, 4, 8, 128), F32),
            pltpu.VMEM((2, 4, 8, 128), F32),
            pltpu.VMEM((2, 2, 4, 8, 128), F32),
            pltpu.VMEM((2, 16, 128), F32),
            pltpu.VMEM((2, 3, 3, 16, 128), F32),
            pltpu.VMEM((8, 8, 128), F32),
            pltpu.VMEM((16, 8, 128), F32),
            dma((8,)), dma((1,)), dma((1,)), dma((2,)),
            dma((6,)), dma((6,)),
            dma((8,)), dma((8,)), dma((16,)), dma((16,)),
            dma((128,)), dma((128,)),
            dma((26,)), dma((26,)),
            dma((8,)), dma((8,)), dma((16,)), dma((16,)),
        ],
        compiler_params=pltpu.CompilerParams(
            collective_id=0, has_side_effects=True, vmem_limit_bytes=48 * 2**20
        ),
        cost_estimate=pl.CostEstimate(flops=2 * 16 * 512 * 128 * 128, bytes_accessed=20 * 2**20, transcendentals=0),
    )(
        old_state,
        remap_weights.reshape(128, 512, 128),
        new_owner.reshape(1, 128),
        new_block.reshape(1, 128),
    )
    return out.reshape(16, 8, 16, 128)


def solution(mesh):
    return jax.shard_map(
        on_device,
        mesh=mesh,
        in_specs=(
            P(None, "gx", "gy", "gz"),
            P(("gx", "gy", "gz"), None, None, None),
            P(("gx", "gy", "gz"), None),
            P(("gx", "gy", "gz")),
        ),
        out_specs=P(None, "gx", "gy", "gz"),
        check_vma=False,
    )
```

```python
import jax
import jax.numpy as jnp
import numpy as np
from jax import lax
from jax.experimental import pallas as pl
from jax.experimental.pallas import tpu as pltpu
from jax.sharding import PartitionSpec as P

MESH = pl.DeviceIdType.MESH
F32 = jnp.float32
BF16 = jnp.bfloat16
CHUNKS = ((0, 32), (32, 64), (64, 96), (96, 128))


def far_first():
    draws = np.random.RandomState(0).permutation(128)
    cells = [(int(t) // 32, int(t) // 8 % 4, int(t) % 8) for t in draws if t]
    cells.sort(key=lambda o: -(min(o[0], 4 - o[0]) + min(o[1], 4 - o[1]) + min(o[2], 8 - o[2]) / 2))
    order = []
    for a, b, c in cells:
        for offset in ((a, b, c), (-a % 4, -b % 4, -c % 8)):
            if offset not in order:
                order.append(offset)
    return order + [(0, 0, 0)]


OFFSETS = far_first()


def limit(below, above):
    return jnp.maximum(jnp.minimum(below, above), 0.0) + jnp.minimum(jnp.maximum(below, above), 0.0)


def kernel(
    state, weights, owner_in, block_in, out,
    w, nat, owner, block, pad, zsend, zrecv, contrib, sendbuf, recvbuf, meta, metat, slotv, slots, lhs, rhs, fields, rim,
    xrecv, ysend, yrecv, erecv, zcol, zcolr, max1, max2,
    lines_sem, w_sem, in_sem, slot_sem, out_sem, halo_s, halo_r, m1_s, m1_r, m2_s, m2_r, a2a_s, a2a_r, rim_s, rim_r,
    x1_s, x1_r, x2_s, x2_r,
):
    gx, gy, gz = lax.axis_index("gx"), lax.axis_index("gy"), lax.axis_index("gz")
    plane = gx * 4 + gy
    me = plane * 8 + gz

    def at(a, b, c):
        return (lax.rem(gx + a % 4, 4), lax.rem(gy + b % 4, 4), lax.rem(gz + c % 8, 8))

    def remote(src, dst, send, recv, device):
        return pltpu.make_async_remote_copy(
            src_ref=src, dst_ref=dst, send_sem=send, recv_sem=recv, device_id=device, device_id_type=MESH
        )

    load_state = pltpu.make_async_copy(state, nat, in_sem.at[0])
    load_owner = pltpu.make_async_copy(owner_in, owner, in_sem.at[1])
    load_block = pltpu.make_async_copy(block_in, block, in_sem.at[2])
    for copy in (load_owner, load_block, load_state):
        copy.start()

    def load_weights(x):
        return pltpu.make_async_copy(weights.at[pl.ds(x * 16, 16)], w.at[pl.ds(x * 16, 16)], w_sem.at[x])

    barrier = pltpu.get_barrier_semaphore()


    def greet_line(c, carry):
        pl.semaphore_signal(barrier, inc=1, device_id=(gx, gy, lax.rem(gz + c, 8)), device_id_type=MESH)
        return carry

    def greet_plane(semaphore):
        def body(e, carry):
            to = lax.rem(plane + e, 16)
            pl.semaphore_signal(semaphore, inc=1, device_id=(lax.div(to, 4), lax.rem(to, 4), gz), device_id_type=MESH)
            return carry
        lax.fori_loop(1, 16, body, 0)

    greet_plane(barrier)
    lax.fori_loop(1, 8, greet_line, 0)

    load_state.wait()
    lane16 = lax.broadcasted_iota(jnp.int32, (16, 128), 1)

    def to_blocks(x, carry):
        low, high = carry
        for part in range(2):
            for half in range(2):
                tile = nat[pl.ds(half * 8, 8), x, pl.ds(part * 8, 8), :]
                pad[x + 1, pl.ds(1 + part * 8, 8), pl.ds(half * 8, 8), :] = jnp.swapaxes(tile, 0, 1)
        for y in range(16):
            b = x * 16 + y
            rolled = pltpu.roll(pad[x + 1, y + 1], b, 1)
            low = jnp.where(lane16 == b, rolled, low)
            high = jnp.where(lane16 == (b + 127) % 128, rolled, high)
        return low, high

    zeros = jnp.zeros((16, 128), F32)
    low, high = lax.fori_loop(0, 8, to_blocks, (zeros, zeros))
    zsend[0] = low
    zsend[1] = pltpu.roll(high, 1, 1)
    pl.semaphore_wait(barrier, 22)

    z_up = remote(zsend.at[1], zrecv.at[0], halo_s.at[0], halo_r.at[0], at(0, 0, 1))
    z_down = remote(zsend.at[0], zrecv.at[1], halo_s.at[1], halo_r.at[1], at(0, 0, -1))
    inner = pl.ds(1, 16)
    cells = pl.ds(1, 8)
    x_up = remote(pad.at[8, inner], pad.at[0, inner], halo_s.at[2], halo_r.at[2], at(1, 0, 0))
    x_down = remote(pad.at[1, inner], pad.at[9, inner], halo_s.at[3], halo_r.at[3], at(-1, 0, 0))
    y_up = remote(pad.at[cells, 16], pad.at[cells, 0], halo_s.at[4], halo_r.at[4], at(0, 1, 0))
    y_down = remote(pad.at[cells, 1], pad.at[cells, 17], halo_s.at[5], halo_r.at[5], at(0, -1, 0))
    for copy in (z_up, z_down, x_up, x_down, y_up, y_down):
        copy.start()

    def meta_one(c):
        mine = meta.at[plane, gz]
        return remote(mine, mine, m1_s.at[c], m1_r.at[c], (gx, gy, lax.rem(gz + c, 8)))

    def meta_two(e):
        to = lax.rem(plane + e, 16)
        return remote(meta.at[plane], meta.at[plane], m2_s.at[e], m2_r.at[e], (lax.div(to, 4), lax.rem(to, 4), gz))

    def start_all(make, lo, hi):
        def body(i, carry):
            make(i).start()
            return carry
        lax.fori_loop(lo, hi, body, 0)

    def recv_all(make, lo, hi):
        def body(i, carry):
            make(i).wait_recv()
            return carry
        lax.fori_loop(lo, hi, body, 0)

    def sent_all(make, lo, hi):
        def body(i, carry):
            make(i).wait_send()
            return carry
        lax.fori_loop(lo, hi, body, 0)

    for x in (1, 2, 3, 4, 5, 6, 0, 7):
        load_weights(x).start()

    greet_plane(lines_sem)
    load_owner.wait()
    load_block.wait()
    meta[plane, gz] = jnp.concatenate([owner[...], block[...]], axis=0)
    start_all(meta_one, 1, 8)

    z_up.wait_recv()
    z_down.wait_recv()
    z_low = jnp.where(gz == 0, 0.0, zrecv[0])
    z_high = jnp.where(gz == 7, 0.0, zrecv[1])

    def contribute(x, y):
        b = (x - 1) * 16 + (y - 1)
        q = pad[x, y]
        before = jnp.where(lane16 == 0, pltpu.roll(z_low, (128 - b) % 128, 1), pltpu.roll(q, 1, 1))
        after = jnp.where(lane16 == 127, pltpu.roll(z_high, 127 - b, 1), pltpu.roll(q, 127, 1))
        moments = jnp.concatenate(
            [
                q,
                limit(q - pad[x - 1, y], pad[x + 1, y] - q),
                limit(q - pad[x, y - 1], pad[x, y + 1] - q),
                limit(q - before, after - q),
            ],
            axis=1,
        ).astype(BF16)
        contrib[b] = jnp.dot(moments, w[b], preferred_element_type=F32)

    def inner_plane(x, carry):
        load_weights(x - 1).wait()
        for y in range(2, 16):
            contribute(x, y)
        return carry

    lax.fori_loop(2, 8, inner_plane, 0)
    lane = lax.broadcasted_iota(jnp.int32, (128, 128), 1)
    sub = lax.broadcasted_iota(jnp.int32, (128, 128), 0)
    named = jnp.broadcast_to(owner[...], (128, 128)).T == lane
    first = jnp.min(jnp.where(named, sub, 128), axis=0, keepdims=True)
    last = jnp.max(jnp.where(named, sub, -1), axis=0, keepdims=True)
    slotv[...] = jnp.concatenate([first, jnp.where(last > first, last, 128)] * 4, axis=0)
    fetch_slots = pltpu.make_async_copy(slotv, slots, slot_sem.at[0])
    fetch_slots.start()
    contrib[128] = jnp.zeros((16, 128), F32)
    for copy in (x_up, x_down, y_up, y_down):
        copy.wait_recv()

    @pl.when(gx == 0)
    def _():
        pad[0, 1:17] = jnp.zeros((16, 16, 128), F32)

    @pl.when(gx == 3)
    def _():
        pad[9, 1:17] = jnp.zeros((16, 16, 128), F32)

    @pl.when(gy == 0)
    def _():
        pad[1:9, 0] = jnp.zeros((8, 16, 128), F32)

    @pl.when(gy == 3)
    def _():
        pad[1:9, 17] = jnp.zeros((8, 16, 128), F32)

    def side_columns(x, carry):
        contribute(x, 1)
        contribute(x, 16)
        return carry

    lax.fori_loop(2, 8, side_columns, 0)
    load_weights(0).wait()
    load_weights(7).wait()

    def side_planes(side, carry):
        for y in range(1, 17):
            contribute(1 + side * 7, y)
        return carry

    lax.fori_loop(0, 2, side_planes, 0)
    fetch_slots.wait()
    pl.semaphore_wait(lines_sem, 15)

    def delivery(i, device):
        return remote(sendbuf.at[i], recvbuf.at[i], a2a_s.at[i], a2a_r.at[i], device)

    def any_delivery(i):
        return delivery(i, at(0, 0, 1))

    for i, offset in enumerate(OFFSETS):
        device = at(*offset)
        to = device[0] * 32 + device[1] * 8 + device[2]
        for slot in range(2):
            held = contrib[jnp.clip(slots[slot, to], 0, 128)]
            if i == 127:
                recvbuf[i, slot] = held
            else:
                sendbuf[i, slot] = held
        if i < 127:
            delivery(i, device).start()
        if i == 15:
            recv_all(meta_one, 1, 8)
            start_all(meta_two, 1, 16)

    recv_all(meta_two, 1, 16)

    for i, (a, b, c) in enumerate(OFFSETS):
        x, y, z = at(-a, -b, -c)
        row = meta[x * 4 + y, z]
        metat[0, i : i + 1, :] = row[0:1]
        metat[1, i : i + 1, :] = row[1:2]
    mine = metat[0] == me
    target = metat[1].astype(F32)
    lane = lane.astype(F32)
    first = jnp.min(jnp.where(mine, lane, 128.0), axis=1, keepdims=True)
    last = jnp.max(jnp.where(mine, lane, -1.0), axis=1, keepdims=True)
    target_0 = jnp.max(jnp.where(mine & (lane == first), target, -1.0), axis=1, keepdims=True)
    target_1 = jnp.max(jnp.where(mine & (lane == last) & (last > first), target, -1.0), axis=1, keepdims=True)
    hot_0 = jnp.where(target_0 == lane, 1.0, 0.0)
    hot_1 = jnp.where(target_1 == lane, 1.0, 0.0)
    for chunk, (start, stop) in enumerate(CHUNKS):
        rows = slice(start, stop)
        both = jnp.concatenate([hot_0[rows], hot_1[rows], hot_0[rows], hot_1[rows]], axis=0)
        lhs[chunk] = both.T.astype(BF16)

    for chunk, (start, stop) in enumerate(CHUNKS):
        steps = stop - start
        recv_all(any_delivery, start, min(stop, 127))
        for part in range(steps // 16):
            for slot in range(2):
                for half in range(2):
                    tile = recvbuf[pl.ds(start + part * 16, 16), slot, pl.ds(half * 8, 8), :]
                    tile = jnp.swapaxes(tile, 0, 1)
                    upper = tile.astype(BF16)
                    lower = (tile - upper.astype(F32)).astype(BF16)
                    row = slot * steps + part * 16
                    rhs[pl.ds(half * 8, 8), pl.ds(row, 16), :] = upper
                    rhs[pl.ds(half * 8, 8), pl.ds(2 * steps + row, 16), :] = lower
        for f in range(16):
            part_sum = jnp.dot(lhs[chunk], rhs[f], preferred_element_type=F32)
            fields[f] = part_sum if chunk == 0 else fields[f] + part_sum

    square = fields[4] * fields[4] + (fields[1] * fields[1] + fields[2] * fields[2] + fields[3] * fields[3])
    max1[gz] = jnp.max(square.reshape(16, 8, 128), axis=0)

    def speed_one(c):
        mine = max1.at[gz]
        return remote(mine, mine, x1_s.at[c], x1_r.at[c], (gx, gy, lax.rem(gz + c, 8)))

    def speed_two(e):
        to = lax.rem(plane + e, 16)
        return remote(max2.at[plane], max2.at[plane], x2_s.at[e], x2_r.at[e], (lax.div(to, 4), lax.rem(to, 4), gz))

    start_all(speed_one, 1, 8)
    store_rest = pltpu.make_async_copy(fields.at[pl.ds(5, 11)], out.at[pl.ds(5, 11)], out_sem.at[0])
    store_rest.start()

    rim_copies = []

    def rim_send(src, dst, device):
        k = len(rim_copies)
        copy = remote(src, dst, rim_s.at[k], rim_r.at[k], device)
        copy.start()
        rim_copies.append(copy)

    rim_send(fields.at[pl.ds(0, 4), pl.ds(112, 16)], xrecv.at[0], at(1, 0, 0))
    rim_send(fields.at[pl.ds(0, 4), pl.ds(0, 16)], xrecv.at[1], at(-1, 0, 0))
    for f in range(4):
        planes = fields[f].reshape(8, 16, 128)
        ysend[0, f] = planes[:, 0]
        ysend[1, f] = planes[:, 15]
    rim_send(ysend.at[1], yrecv.at[0], at(0, 1, 0))
    rim_send(ysend.at[0], yrecv.at[1], at(0, -1, 0))
    for dx in (1, -1):
        for dy in (1, -1):
            rim_send(ysend.at[(1 + dy) // 2], erecv.at[(1 - dx) // 2, (1 - dy) // 2], at(dx, dy, 0))

    def columns(x, carry):
        low, high = carry
        for f in range(4):
            l = (x + 1) * 4 + f
            rolled = pltpu.roll(fields[f, pl.ds(pl.multiple_of(x * 16, 16), 16), :], l, 1)
            low = jnp.where(lane16 == l, rolled, low)
            high = jnp.where(lane16 == l - 1, rolled, high)
        return low, high

    low, high = lax.fori_loop(0, 8, columns, (zeros, zeros))
    zcol[0] = low
    zcol[1] = pltpu.roll(high, 1, 1)
    for dx in (0, 1, -1):
        for dy in (0, 1, -1):
            rim_send(zcol.at[1], zcolr.at[0, 1 - dx, 1 - dy], at(dx, dy, 1))
            rim_send(zcol.at[0], zcolr.at[1, 1 - dx, 1 - dy], at(dx, dy, -1))

    recv_all(speed_one, 1, 8)
    max2[plane] = jnp.max(max1[...], axis=0)
    start_all(speed_two, 1, 16)

    for copy in rim_copies:
        copy.wait_recv()
    sub8 = lax.broadcasted_iota(jnp.int32, (8, 128), 0)
    no_xl, no_xh = gx == 0, gx == 3
    no_yl, no_yh = gy == 0, gy == 3

    def tail(above, below):
        above = jnp.where(no_yh, 0.0, above)
        below = jnp.where(no_yl, 0.0, below)
        return jnp.where(sub8 == 7, below, above)

    def row(ref, *index):
        return jnp.broadcast_to(ref[index], (8, 128))

    def padded(f, x):
        if 1 <= x <= 8:
            cells = fields[f, (x - 1) * 16 : x * 16]
            edge = slice(x - 1, x)
            return jnp.concatenate([cells, tail(row(yrecv, 1, f, edge), row(yrecv, 0, f, edge))], axis=0)
        side, none, edge = (0, no_xl, slice(7, 8)) if x == 0 else (1, no_xh, slice(0, 1))
        rows = tail(row(erecv, side, 1, f, edge), row(erecv, side, 0, f, edge))
        return jnp.where(none, 0.0, jnp.concatenate([xrecv[side, f], rows], axis=0))

    lane24 = lax.broadcasted_iota(jnp.int32, (24, 128), 1)

    def gathered(side, none):
        tiles = []
        for dx in range(3):
            tiles.append(
                jnp.concatenate(
                    [zcolr[side, dx, 1], tail(zcolr[side, dx, 2, 0:8], zcolr[side, dx, 0, 8:16])], axis=0
                )
            )
        below = jnp.where(no_xl, 0.0, pltpu.roll(tiles[0], 96, 1))
        above = jnp.where(no_xh, 0.0, pltpu.roll(tiles[2], 32, 1))
        whole = jnp.where(lane24 < 4, below, jnp.where(lane24 < 36, tiles[1], above))
        return jnp.where(none, 0.0, whole)

    z_low = gathered(0, gz == 0)
    z_high = gathered(1, gz == 7)

    def along_z(f, x):
        q = padded(f, x)
        l = x * 4 + f
        before = jnp.where(lane24 == 0, pltpu.roll(z_low, (128 - l) % 128, 1), pltpu.roll(q, 1, 1))
        after = jnp.where(lane24 == 127, pltpu.roll(z_high, 127 - l, 1), pltpu.roll(q, 127, 1))
        return before + 2.0 * q + after, after - before

    def smooth_y(v):
        return (pltpu.roll(v, 1, 0) + 2.0 * v + pltpu.roll(v, 23, 0))[0:16]

    def spread_y(v):
        return (pltpu.roll(v, 23, 0) - pltpu.roll(v, 1, 0))[0:16]

    def plane_terms(x):
        p_s, p_d = along_z(0, x)
        u_s, _ = along_z(1, x)
        v_s, _ = along_z(2, x)
        _, w_d = along_z(3, x)
        return (
            smooth_y(p_s), spread_y(p_s), smooth_y(p_d),
            smooth_y(u_s), spread_y(v_s) + smooth_y(w_d),
        )

    terms = [plane_terms(0), plane_terms(1)]
    for x in range(8):
        terms.append(plane_terms(x + 2))
        before, here, after = terms[x : x + 3]
        gradient = (
            after[0] - before[0],
            before[1] + 2.0 * here[1] + after[1],
            before[2] + 2.0 * here[2] + after[2],
        )
        divergence = after[3] - before[3] + (before[4] + 2.0 * here[4] + after[4])
        rim[3, x] = divergence * (1.0 / 32.0)
        for k in range(3):
            rim[k, x] = gradient[k] * (1.0 / 32.0)

    for copy in rim_copies:
        copy.wait_send()
    recv_all(speed_two, 1, 16)
    largest = jnp.max(jnp.max(max2[...], axis=0), axis=(0, 1), keepdims=True)
    step = 0.5 / jnp.sqrt(1.0 + 0.05 * largest)
    step = jnp.broadcast_to(step, (16, 128))

    def advance(x):
        rows = slice(x * 16, x * 16 + 16)
        divergence = rim[3, x]
        pressure = fields[0, rows]
        fields[4, rows] = fields[4, rows] - step * pressure * divergence
        fields[0, rows] = pressure - step * divergence
        for k in range(3):
            fields[1 + k, rows] = fields[1 + k, rows] - step * rim[k, x]

    for x in range(8):
        advance(x)
    store = pltpu.make_async_copy(fields.at[pl.ds(0, 5)], out.at[pl.ds(0, 5)], out_sem.at[1])
    store.start()
    for copy in (z_up, z_down, x_up, x_down, y_up, y_down):
        copy.wait_send()
    sent_all(meta_one, 1, 8)
    sent_all(meta_two, 1, 16)
    sent_all(any_delivery, 0, 127)
    sent_all(speed_one, 1, 8)
    sent_all(speed_two, 1, 16)
    store_rest.wait()
    store.wait()


def on_device(old_state, remap_weights, new_owner, new_block):
    dma = pltpu.SemaphoreType.DMA
    hbm = pl.BlockSpec(memory_space=pltpu.HBM)
    out = pl.pallas_call(
        kernel,
        out_shape=jax.ShapeDtypeStruct((16, 128, 128), F32),
        in_specs=[hbm, hbm, hbm, hbm],
        out_specs=hbm,
        scratch_shapes=[
            pltpu.VMEM((128, 512, 128), BF16),
            pltpu.VMEM((16, 8, 16, 128), F32),
            pltpu.VMEM((1, 128), jnp.int32),
            pltpu.VMEM((1, 128), jnp.int32),
            pltpu.VMEM((10, 18, 16, 128), F32),
            pltpu.VMEM((2, 16, 128), F32),
            pltpu.VMEM((2, 16, 128), F32),
            pltpu.VMEM((129, 16, 128), F32),
            pltpu.VMEM((128, 2, 16, 128), F32),
            pltpu.VMEM((128, 2, 16, 128), F32),
            pltpu.VMEM((16, 8, 2, 128), jnp.int32),
            pltpu.VMEM((2, 128, 128), jnp.int32),
            pltpu.VMEM((8, 128), jnp.int32),
            pltpu.SMEM((8, 128), jnp.int32),
            pltpu.VMEM((len(CHUNKS), 128, 128), BF16),
            pltpu.VMEM((16, 128, 128), BF16),
            pltpu.VMEM((16, 128, 128), F32),
            pltpu.VMEM((4, 8, 16, 128), F32),
            pltpu.VMEM((2, 4, 16, 128), F32),
            pltpu.VMEM((2, 4, 8, 128), F32),
            pltpu.VMEM((2, 4, 8, 128), F32),
            pltpu.VMEM((2, 2, 4, 8, 128), F32),
            pltpu.VMEM((2, 16, 128), F32),
            pltpu.VMEM((2, 3, 3, 16, 128), F32),
            pltpu.VMEM((8, 8, 128), F32),
            pltpu.VMEM((16, 8, 128), F32),
            pltpu.SemaphoreType.REGULAR,
            dma((8,)), dma((3,)), dma((1,)), dma((2,)),
            dma((6,)), dma((6,)),
            dma((8,)), dma((8,)), dma((16,)), dma((16,)),
            dma((128,)), dma((128,)),
            dma((26,)), dma((26,)),
            dma((8,)), dma((8,)), dma((16,)), dma((16,)),
        ],
        compiler_params=pltpu.CompilerParams(
            collective_id=0, has_side_effects=True, vmem_limit_bytes=60 * 2**20
        ),
        cost_estimate=pl.CostEstimate(flops=2 * 16 * 512 * 128 * 128, bytes_accessed=20 * 2**20, transcendentals=0),
    )(
        old_state,
        remap_weights.reshape(128, 512, 128),
        new_owner.reshape(1, 128),
        new_block.reshape(1, 128),
    )
    return out.reshape(16, 8, 16, 128)


def solution(mesh):
    return jax.shard_map(
        on_device,
        mesh=mesh,
        in_specs=(
            P(None, "gx", "gy", "gz"),
            P(("gx", "gy", "gz"), None, None, None),
            P(("gx", "gy", "gz"), None),
            P(("gx", "gy", "gz")),
        ),
        out_specs=P(None, "gx", "gy", "gz"),
        check_vma=False,
    )
```

```python
import jax
import jax.numpy as jnp
import numpy as np
from jax import lax
from jax.experimental import pallas as pl
from jax.experimental.pallas import tpu as pltpu
from jax.sharding import PartitionSpec as P

MESH = pl.DeviceIdType.MESH
F32 = jnp.float32
BF16 = jnp.bfloat16
CHUNKS = 4
STEPS = 128 // CHUNKS
HALO_Z, HALO, META_LINE, META_PLANE, RIM, SPEED_PLANE, SPEED_LINE, DELIVERY = range(8)


def far_first():
    draws = np.random.RandomState(0).permutation(128)
    cells = [(int(t) // 32, int(t) // 8 % 4, int(t) % 8) for t in draws if t]
    cells.sort(key=lambda o: -(min(o[0], 4 - o[0]) + min(o[1], 4 - o[1]) + min(o[2], 8 - o[2]) / 2))
    order = []
    for a, b, c in cells:
        for offset in ((a, b, c), (-a % 4, -b % 4, -c % 8)):
            if offset not in order:
                order.append(offset)
    return order + [(0, 0, 0)]


OFFSETS = far_first()


def limit(below, above):
    return jnp.maximum(jnp.minimum(below, above), 0.0) + jnp.minimum(jnp.maximum(below, above), 0.0)


def kernel(
    state, weights, owner_in, block_in, out,
    w, nat, owner, block, pad, zsend, zrecv, contrib, sendbuf, recvbuf, meta, metat, slotv, slots, lhs, rhs, fields, rim,
    xrecv, ysend, yrecv, erecv, zcol, zcolr, max1, max2,
    lines_sem, w_sem, in_sem, slot_sem, out_sem, sent, got,
):
    gx, gy, gz = lax.axis_index("gx"), lax.axis_index("gy"), lax.axis_index("gz")
    me = (gx * 4 + gy) * 8 + gz

    def around(here, size):
        steps = [here]
        for step in range(1, size):
            there = here + step
            steps.append(jnp.where(there >= size, there - size, there))
        return steps

    xs, ys, zs = around(gx, 4), around(gy, 4), around(gz, 8)

    def at(a, b, c):
        return xs[a % 4], ys[b % 4], zs[c % 8]

    def remote(src, dst, group, device, part=0):
        return pltpu.make_async_remote_copy(
            src_ref=src, dst_ref=dst, send_sem=sent.at[group], recv_sem=got.at[group + part], device_id=device,
            device_id_type=MESH,
        )

    def received(ref, group, part=0):
        remote(ref, ref, group, at(0, 0, 1), part).wait_recv()

    def delivered(ref, group):
        remote(ref, ref, group, at(0, 0, 1)).wait_send()

    load_state = pltpu.make_async_copy(state, nat, in_sem.at[0])
    load_owner = pltpu.make_async_copy(owner_in, owner, in_sem.at[1])
    load_block = pltpu.make_async_copy(block_in, block, in_sem.at[2])
    for copy in (load_owner, load_block, load_state):
        copy.start()

    def load_weights(x):
        return pltpu.make_async_copy(weights.at[pl.ds(x * 16, 16)], w.at[pl.ds(x * 16, 16)], w_sem.at[x])

    barrier = pltpu.get_barrier_semaphore()


    def greet(semaphore, device):
        pl.semaphore_signal(semaphore, inc=1, device_id=device, device_id_type=MESH)

    plane = [(a, b) for a in range(4) for b in range(4)]
    for a, b in plane[1:]:
        greet(barrier, at(a, b, 0))
    for c in range(1, 8):
        greet(barrier, at(0, 0, c))

    load_state.wait()
    lane16 = lax.broadcasted_iota(jnp.int32, (16, 128), 1)

    def to_blocks(x, carry):
        low, high = carry
        for part in range(2):
            for half in range(2):
                tile = nat[pl.ds(half * 8, 8), x, pl.ds(part * 8, 8), :]
                pad[x + 1, pl.ds(1 + part * 8, 8), pl.ds(half * 8, 8), :] = jnp.swapaxes(tile, 0, 1)
        for y in range(16):
            b = x * 16 + y
            rolled = pltpu.roll(pad[x + 1, y + 1], b, 1)
            low = jnp.where(lane16 == b, rolled, low)
            high = jnp.where(lane16 == (b + 127) % 128, rolled, high)
        return low, high

    zeros = jnp.zeros((16, 128), F32)
    low, high = lax.fori_loop(0, 8, to_blocks, (zeros, zeros))
    zsend[0] = low
    zsend[1] = pltpu.roll(high, 1, 1)
    pl.semaphore_wait(barrier, 22)

    inner = pl.ds(1, 16)
    cells = pl.ds(1, 8)
    remote(zsend.at[1], zrecv.at[0], HALO_Z, at(0, 0, 1)).start()
    remote(zsend.at[0], zrecv.at[1], HALO_Z, at(0, 0, -1)).start()
    remote(pad.at[8, inner], pad.at[0, inner], HALO, at(1, 0, 0)).start()
    remote(pad.at[1, inner], pad.at[9, inner], HALO, at(-1, 0, 0)).start()
    remote(pad.at[cells, 16], pad.at[cells, 0], HALO, at(0, 1, 0)).start()
    remote(pad.at[cells, 1], pad.at[cells, 17], HALO, at(0, -1, 0)).start()
    for x in (1, 2, 3, 4, 5, 6, 0, 7):
        load_weights(x).start()

    for a, b in plane[1:]:
        greet(lines_sem, at(a, b, 0))
    load_owner.wait()
    load_block.wait()
    meta[0, 0] = jnp.concatenate([owner[...], block[...]], axis=0)
    for c in range(1, 8):
        remote(meta.at[0, 0], meta.at[0, c], META_LINE, at(0, 0, c)).start()

    received(zrecv, HALO_Z)
    z_low = jnp.where(gz == 0, 0.0, zrecv[0])
    z_high = jnp.where(gz == 7, 0.0, zrecv[1])

    def contribute(x, y):
        b = (x - 1) * 16 + (y - 1)
        q = pad[x, y]
        before = jnp.where(lane16 == 0, pltpu.roll(z_low, (128 - b) % 128, 1), pltpu.roll(q, 1, 1))
        after = jnp.where(lane16 == 127, pltpu.roll(z_high, 127 - b, 1), pltpu.roll(q, 127, 1))
        moments = jnp.concatenate(
            [
                q,
                limit(q - pad[x - 1, y], pad[x + 1, y] - q),
                limit(q - pad[x, y - 1], pad[x, y + 1] - q),
                limit(q - before, after - q),
            ],
            axis=1,
        ).astype(BF16)
        contrib[b] = jnp.dot(moments, w[b], preferred_element_type=F32)

    def inner_plane(x, carry):
        load_weights(x - 1).wait()
        for y in range(2, 16):
            contribute(x, y)
        return carry

    lax.fori_loop(2, 8, inner_plane, 0)
    lane = lax.broadcasted_iota(jnp.int32, (128, 128), 1)
    sub = lax.broadcasted_iota(jnp.int32, (128, 128), 0)
    named = jnp.broadcast_to(owner[...], (128, 128)).T == lane
    first = jnp.min(jnp.where(named, sub, 128), axis=0, keepdims=True)
    last = jnp.max(jnp.where(named, sub, -1), axis=0, keepdims=True)
    slotv[...] = jnp.concatenate([first, jnp.where(last > first, last, 128)] * 4, axis=0)
    fetch_slots = pltpu.make_async_copy(slotv, slots, slot_sem.at[0])
    fetch_slots.start()
    contrib[128] = jnp.zeros((16, 128), F32)
    received(pad.at[0:3, inner], HALO)

    @pl.when(gx == 0)
    def _():
        pad[0, 1:17] = jnp.zeros((16, 16, 128), F32)

    @pl.when(gx == 3)
    def _():
        pad[9, 1:17] = jnp.zeros((16, 16, 128), F32)

    @pl.when(gy == 0)
    def _():
        pad[1:9, 0] = jnp.zeros((8, 16, 128), F32)

    @pl.when(gy == 3)
    def _():
        pad[1:9, 17] = jnp.zeros((8, 16, 128), F32)

    def side_columns(x, carry):
        contribute(x, 1)
        contribute(x, 16)
        return carry

    lax.fori_loop(2, 8, side_columns, 0)
    load_weights(0).wait()
    load_weights(7).wait()

    def side_planes(side, carry):
        for y in range(1, 17):
            contribute(1 + side * 7, y)
        return carry

    lax.fori_loop(0, 2, side_planes, 0)
    fetch_slots.wait()
    pl.semaphore_wait(lines_sem, 15)

    for i, offset in enumerate(OFFSETS):
        device = at(*offset)
        to = device[0] * 32 + device[1] * 8 + device[2]
        for slot in range(2):
            held = contrib[jnp.clip(slots[slot, to], 0, 128)]
            if i == 127:
                recvbuf[i, slot] = held
            else:
                sendbuf[i, slot] = held
        if i < 127:
            remote(sendbuf.at[i], recvbuf.at[i], DELIVERY, device, i // STEPS).start()
        if i == 15:
            received(meta.at[0, 1:8], META_LINE)
            for k, (a, b) in enumerate(plane[1:]):
                remote(meta.at[0], meta.at[k + 1], META_PLANE, at(a, b, 0)).start()

    received(meta.at[1:16], META_PLANE)
    for i, (a, b, c) in enumerate(OFFSETS):
        row = meta[a * 4 + b, c]
        metat[0, i : i + 1, :] = row[0:1]
        metat[1, i : i + 1, :] = row[1:2]
    mine = metat[0] == me
    target = metat[1].astype(F32)
    lane = lane.astype(F32)
    first = jnp.min(jnp.where(mine, lane, 128.0), axis=1, keepdims=True)
    last = jnp.max(jnp.where(mine, lane, -1.0), axis=1, keepdims=True)
    target_0 = jnp.max(jnp.where(mine & (lane == first), target, -1.0), axis=1, keepdims=True)
    target_1 = jnp.max(jnp.where(mine & (lane == last) & (last > first), target, -1.0), axis=1, keepdims=True)
    hot_0 = jnp.where(target_0 == lane, 1.0, 0.0)
    hot_1 = jnp.where(target_1 == lane, 1.0, 0.0)
    for chunk in range(CHUNKS):
        rows = slice(chunk * STEPS, (chunk + 1) * STEPS)
        both = jnp.concatenate([hot_0[rows], hot_1[rows], hot_0[rows], hot_1[rows]], axis=0)
        lhs[chunk] = both.T.astype(BF16)

    for chunk in range(CHUNKS):
        start = chunk * STEPS
        received(recvbuf.at[start : min(start + STEPS, 127)], DELIVERY, chunk)
        for part in range(STEPS // 16):
            for slot in range(2):
                for half in range(2):
                    tile = recvbuf[pl.ds(start + part * 16, 16), slot, pl.ds(half * 8, 8), :]
                    tile = jnp.swapaxes(tile, 0, 1)
                    upper = tile.astype(BF16)
                    lower = (tile - upper.astype(F32)).astype(BF16)
                    row = slot * STEPS + part * 16
                    rhs[pl.ds(half * 8, 8), pl.ds(row, 16), :] = upper
                    rhs[pl.ds(half * 8, 8), pl.ds(2 * STEPS + row, 16), :] = lower
        for f in range(16):
            part_sum = jnp.dot(lhs[chunk], rhs[f], preferred_element_type=F32)
            fields[f] = part_sum if chunk == 0 else fields[f] + part_sum

    square = fields[4] * fields[4] + (fields[1] * fields[1] + fields[2] * fields[2] + fields[3] * fields[3])
    max1[0] = jnp.max(square.reshape(16, 8, 128), axis=0)
    for k, (a, b) in enumerate(plane[1:]):
        remote(max1.at[0], max1.at[k + 1], SPEED_PLANE, at(a, b, 0)).start()
    store_rest = pltpu.make_async_copy(fields.at[pl.ds(5, 11)], out.at[pl.ds(5, 11)], out_sem.at[0])
    store_rest.start()

    def rim_send(src, dst, device):
        remote(src, dst, RIM, device).start()

    rim_send(fields.at[pl.ds(0, 4), pl.ds(112, 16)], xrecv.at[0], at(1, 0, 0))
    rim_send(fields.at[pl.ds(0, 4), pl.ds(0, 16)], xrecv.at[1], at(-1, 0, 0))
    for f in range(4):
        planes = fields[f].reshape(8, 16, 128)
        ysend[0, f] = planes[:, 0]
        ysend[1, f] = planes[:, 15]
    rim_send(ysend.at[1], yrecv.at[0], at(0, 1, 0))
    rim_send(ysend.at[0], yrecv.at[1], at(0, -1, 0))
    for dx in (1, -1):
        for dy in (1, -1):
            rim_send(ysend.at[(1 + dy) // 2], erecv.at[(1 - dx) // 2, (1 - dy) // 2], at(dx, dy, 0))

    def columns(x, carry):
        low, high = carry
        for f in range(4):
            l = (x + 1) * 4 + f
            rolled = pltpu.roll(fields[f, pl.ds(pl.multiple_of(x * 16, 16), 16), :], l, 1)
            low = jnp.where(lane16 == l, rolled, low)
            high = jnp.where(lane16 == l - 1, rolled, high)
        return low, high

    low, high = lax.fori_loop(0, 8, columns, (zeros, zeros))
    zcol[0] = low
    zcol[1] = pltpu.roll(high, 1, 1)
    for dx in (0, 1, -1):
        for dy in (0, 1, -1):
            rim_send(zcol.at[1], zcolr.at[0, 1 - dx, 1 - dy], at(dx, dy, 1))
            rim_send(zcol.at[0], zcolr.at[1, 1 - dx, 1 - dy], at(dx, dy, -1))

    received(max1.at[1:16], SPEED_PLANE)
    max2[0] = jnp.max(max1[...], axis=0)
    for c in range(1, 8):
        remote(max2.at[0], max2.at[c], SPEED_LINE, at(0, 0, c)).start()

    received(contrib.at[0:38], RIM)
    sub8 = lax.broadcasted_iota(jnp.int32, (8, 128), 0)
    no_xl, no_xh = gx == 0, gx == 3
    no_yl, no_yh = gy == 0, gy == 3

    def tail(above, below):
        above = jnp.where(no_yh, 0.0, above)
        below = jnp.where(no_yl, 0.0, below)
        return jnp.where(sub8 == 7, below, above)

    def row(ref, *index):
        return jnp.broadcast_to(ref[index], (8, 128))

    def padded(f, x):
        if 1 <= x <= 8:
            cells = fields[f, (x - 1) * 16 : x * 16]
            edge = slice(x - 1, x)
            return jnp.concatenate([cells, tail(row(yrecv, 1, f, edge), row(yrecv, 0, f, edge))], axis=0)
        side, none, edge = (0, no_xl, slice(7, 8)) if x == 0 else (1, no_xh, slice(0, 1))
        rows = tail(row(erecv, side, 1, f, edge), row(erecv, side, 0, f, edge))
        return jnp.where(none, 0.0, jnp.concatenate([xrecv[side, f], rows], axis=0))

    lane24 = lax.broadcasted_iota(jnp.int32, (24, 128), 1)

    def gathered(side, none):
        tiles = []
        for dx in range(3):
            tiles.append(
                jnp.concatenate(
                    [zcolr[side, dx, 1], tail(zcolr[side, dx, 2, 0:8], zcolr[side, dx, 0, 8:16])], axis=0
                )
            )
        below = jnp.where(no_xl, 0.0, pltpu.roll(tiles[0], 96, 1))
        above = jnp.where(no_xh, 0.0, pltpu.roll(tiles[2], 32, 1))
        whole = jnp.where(lane24 < 4, below, jnp.where(lane24 < 36, tiles[1], above))
        return jnp.where(none, 0.0, whole)

    z_low = gathered(0, gz == 0)
    z_high = gathered(1, gz == 7)

    def along_z(f, x):
        q = padded(f, x)
        l = x * 4 + f
        before = jnp.where(lane24 == 0, pltpu.roll(z_low, (128 - l) % 128, 1), pltpu.roll(q, 1, 1))
        after = jnp.where(lane24 == 127, pltpu.roll(z_high, 127 - l, 1), pltpu.roll(q, 127, 1))
        return before + 2.0 * q + after, after - before

    def smooth_y(v):
        return (pltpu.roll(v, 1, 0) + 2.0 * v + pltpu.roll(v, 23, 0))[0:16]

    def spread_y(v):
        return (pltpu.roll(v, 23, 0) - pltpu.roll(v, 1, 0))[0:16]

    def plane_terms(x):
        p_s, p_d = along_z(0, x)
        u_s, _ = along_z(1, x)
        v_s, _ = along_z(2, x)
        _, w_d = along_z(3, x)
        return (
            smooth_y(p_s), spread_y(p_s), smooth_y(p_d),
            smooth_y(u_s), spread_y(v_s) + smooth_y(w_d),
        )

    terms = [plane_terms(0), plane_terms(1)]
    for x in range(8):
        terms.append(plane_terms(x + 2))
        before, here, after = terms[x : x + 3]
        gradient = (
            after[0] - before[0],
            before[1] + 2.0 * here[1] + after[1],
            before[2] + 2.0 * here[2] + after[2],
        )
        divergence = after[3] - before[3] + (before[4] + 2.0 * here[4] + after[4])
        rim[3, x] = divergence * (1.0 / 32.0)
        for k in range(3):
            rim[k, x] = gradient[k] * (1.0 / 32.0)

    delivered(contrib.at[0:38], RIM)
    received(max2.at[1:8], SPEED_LINE)
    largest = jnp.max(jnp.max(max2[...], axis=0), axis=(0, 1), keepdims=True)
    step = 0.5 / jnp.sqrt(1.0 + 0.05 * largest)
    step = jnp.broadcast_to(step, (16, 128))

    def advance(x):
        rows = slice(x * 16, x * 16 + 16)
        divergence = rim[3, x]
        pressure = fields[0, rows]
        fields[4, rows] = fields[4, rows] - step * pressure * divergence
        fields[0, rows] = pressure - step * divergence
        for k in range(3):
            fields[1 + k, rows] = fields[1 + k, rows] - step * rim[k, x]

    for x in range(8):
        advance(x)
    store = pltpu.make_async_copy(fields.at[pl.ds(0, 5)], out.at[pl.ds(0, 5)], out_sem.at[1])
    store.start()
    delivered(zsend, HALO_Z)
    delivered(pad.at[0:3, inner], HALO)
    delivered(meta.at[0, 1:8], META_LINE)
    delivered(meta.at[1:16], META_PLANE)
    delivered(sendbuf.at[0:127], DELIVERY)
    delivered(max1.at[1:16], SPEED_PLANE)
    delivered(max2.at[1:8], SPEED_LINE)
    store_rest.wait()
    store.wait()


def on_device(old_state, remap_weights, new_owner, new_block):
    dma = pltpu.SemaphoreType.DMA
    hbm = pl.BlockSpec(memory_space=pltpu.HBM)
    out = pl.pallas_call(
        kernel,
        out_shape=jax.ShapeDtypeStruct((16, 128, 128), F32),
        in_specs=[hbm, hbm, hbm, hbm],
        out_specs=hbm,
        scratch_shapes=[
            pltpu.VMEM((128, 512, 128), BF16),
            pltpu.VMEM((16, 8, 16, 128), F32),
            pltpu.VMEM((1, 128), jnp.int32),
            pltpu.VMEM((1, 128), jnp.int32),
            pltpu.VMEM((10, 18, 16, 128), F32),
            pltpu.VMEM((2, 16, 128), F32),
            pltpu.VMEM((2, 16, 128), F32),
            pltpu.VMEM((129, 16, 128), F32),
            pltpu.VMEM((128, 2, 16, 128), F32),
            pltpu.VMEM((128, 2, 16, 128), F32),
            pltpu.VMEM((16, 8, 2, 128), jnp.int32),
            pltpu.VMEM((2, 128, 128), jnp.int32),
            pltpu.VMEM((8, 128), jnp.int32),
            pltpu.SMEM((8, 128), jnp.int32),
            pltpu.VMEM((CHUNKS, 128, 128), BF16),
            pltpu.VMEM((16, 128, 128), BF16),
            pltpu.VMEM((16, 128, 128), F32),
            pltpu.VMEM((4, 8, 16, 128), F32),
            pltpu.VMEM((2, 4, 16, 128), F32),
            pltpu.VMEM((2, 4, 8, 128), F32),
            pltpu.VMEM((2, 4, 8, 128), F32),
            pltpu.VMEM((2, 2, 4, 8, 128), F32),
            pltpu.VMEM((2, 16, 128), F32),
            pltpu.VMEM((2, 3, 3, 16, 128), F32),
            pltpu.VMEM((16, 8, 128), F32),
            pltpu.VMEM((8, 8, 128), F32),
            pltpu.SemaphoreType.REGULAR,
            dma((8,)), dma((3,)), dma((1,)), dma((2,)), dma((8,)), dma((7 + CHUNKS,)),
        ],
        compiler_params=pltpu.CompilerParams(
            collective_id=0, has_side_effects=True, vmem_limit_bytes=60 * 2**20
        ),
        cost_estimate=pl.CostEstimate(flops=2 * 16 * 512 * 128 * 128, bytes_accessed=20 * 2**20, transcendentals=0),
    )(
        old_state,
        remap_weights.reshape(128, 512, 128),
        new_owner.reshape(1, 128),
        new_block.reshape(1, 128),
    )
    return out.reshape(16, 8, 16, 128)


def solution(mesh):
    return jax.shard_map(
        on_device,
        mesh=mesh,
        in_specs=(
            P(None, "gx", "gy", "gz"),
            P(("gx", "gy", "gz"), None, None, None),
            P(("gx", "gy", "gz"), None),
            P(("gx", "gy", "gz")),
        ),
        out_specs=P(None, "gx", "gy", "gz"),
        check_vma=False,
    )
```

```python
import jax
import jax.numpy as jnp
import numpy as np
from jax import lax
from jax.experimental import pallas as pl
from jax.experimental.pallas import tpu as pltpu
from jax.sharding import PartitionSpec as P

MESH = pl.DeviceIdType.MESH
F32 = jnp.float32
BF16 = jnp.bfloat16
CHUNKS = 4
STEPS = 128 // CHUNKS
HALO_Z, HALO, META_LINE, META_PLANE, RIM, SPEED_CORE, SPEED_CHIPS, DELIVERY = range(8)


def far_first():
    draws = np.random.RandomState(0).permutation(128)
    cells = [(int(t) // 32, int(t) // 8 % 4, int(t) % 8) for t in draws if t]
    cells.sort(key=lambda o: -(min(o[0], 4 - o[0]) + min(o[1], 4 - o[1]) + min(o[2], 8 - o[2]) / 2))
    order = []
    for a, b, c in cells:
        for offset in ((a, b, c), (-a % 4, -b % 4, -c % 8)):
            if offset not in order:
                order.append(offset)
    return order + [(0, 0, 0)]


OFFSETS = far_first()


def limit(below, above):
    return jnp.maximum(jnp.minimum(below, above), 0.0) + jnp.minimum(jnp.maximum(below, above), 0.0)


def kernel(
    state, weights, numbers, fields,
    w, nat, pad, zsend, zrecv, contrib, sendbuf, recvbuf, meta, metat, slotv, slots, lhs, rhs, rim,
    xrecv, ysend, yrecv, erecv, zcol, zcolr, max1, max2,
    lines_sem, w_sem, in_sem, slot_sem, sent, got,
):
    gx, gy, gz = lax.axis_index("gx"), lax.axis_index("gy"), lax.axis_index("gz")
    me = (gx * 4 + gy) * 8 + gz

    def around(here, size):
        steps = [here]
        for step in range(1, size):
            there = here + step
            steps.append(jnp.where(there >= size, there - size, there))
        return steps

    xs, ys, zs = around(gx, 4), around(gy, 4), around(gz, 8)

    def at(a, b, c):
        return xs[a % 4], ys[b % 4], zs[c % 8]

    def remote(src, dst, group, device, part=0):
        return pltpu.make_async_remote_copy(
            src_ref=src, dst_ref=dst, send_sem=sent.at[group], recv_sem=got.at[group + part], device_id=device,
            device_id_type=MESH,
        )

    def received(ref, group, part=0):
        remote(ref, ref, group, at(0, 0, 1), part).wait_recv()

    def delivered(ref, group):
        remote(ref, ref, group, at(0, 0, 1)).wait_send()

    load_state = pltpu.make_async_copy(state, nat, in_sem.at[0])
    load_state.start()

    def load_weights(x):
        return pltpu.make_async_copy(weights.at[pl.ds(x * 16, 16)], w.at[pl.ds(x * 16, 16)], w_sem.at[x])

    barrier = pltpu.get_barrier_semaphore()


    def greet(semaphore, device):
        pl.semaphore_signal(semaphore, inc=1, device_id=device, device_id_type=MESH)

    plane = [(a, b) for a in range(4) for b in range(4)]
    for a, b in plane[1:]:
        greet(barrier, at(a, b, 0))
    for c in range(1, 8):
        greet(barrier, at(0, 0, c))

    load_state.wait()
    lane16 = lax.broadcasted_iota(jnp.int32, (16, 128), 1)

    def to_blocks(x, carry):
        low, high = carry
        for part in range(2):
            for half in range(2):
                tile = nat[pl.ds(half * 8, 8), x, pl.ds(part * 8, 8), :]
                pad[x + 1, pl.ds(1 + part * 8, 8), pl.ds(half * 8, 8), :] = jnp.swapaxes(tile, 0, 1)
        for y in range(16):
            b = x * 16 + y
            rolled = pltpu.roll(pad[x + 1, y + 1], b, 1)
            low = jnp.where(lane16 == b, rolled, low)
            high = jnp.where(lane16 == (b + 127) % 128, rolled, high)
        return low, high

    zeros = jnp.zeros((16, 128), F32)
    low, high = lax.fori_loop(0, 8, to_blocks, (zeros, zeros))
    zsend[0] = low
    zsend[1] = pltpu.roll(high, 1, 1)
    pl.semaphore_wait(barrier, 22)

    inner = pl.ds(1, 16)
    cells = pl.ds(1, 8)
    remote(zsend.at[1], zrecv.at[0], HALO_Z, at(0, 0, 1)).start()
    remote(zsend.at[0], zrecv.at[1], HALO_Z, at(0, 0, -1)).start()
    remote(pad.at[8, inner], pad.at[0, inner], HALO, at(1, 0, 0)).start()
    remote(pad.at[1, inner], pad.at[9, inner], HALO, at(-1, 0, 0)).start()
    remote(pad.at[cells, 16], pad.at[cells, 0], HALO, at(0, 1, 0)).start()
    remote(pad.at[cells, 1], pad.at[cells, 17], HALO, at(0, -1, 0)).start()
    for x in (1, 2, 3, 4, 5, 6, 0, 7):
        load_weights(x).start()

    for a, b in plane[1:]:
        greet(lines_sem, at(a, b, 0))
    meta[0, 0] = numbers[...]
    for c in range(1, 8):
        remote(meta.at[0, 0], meta.at[0, c], META_LINE, at(0, 0, c)).start()

    received(zrecv, HALO_Z)
    z_low = jnp.where(gz == 0, 0.0, zrecv[0])
    z_high = jnp.where(gz == 7, 0.0, zrecv[1])

    def contribute(x, y):
        b = (x - 1) * 16 + (y - 1)
        q = pad[x, y]
        before = jnp.where(lane16 == 0, pltpu.roll(z_low, (128 - b) % 128, 1), pltpu.roll(q, 1, 1))
        after = jnp.where(lane16 == 127, pltpu.roll(z_high, 127 - b, 1), pltpu.roll(q, 127, 1))
        moments = jnp.concatenate(
            [
                q,
                limit(q - pad[x - 1, y], pad[x + 1, y] - q),
                limit(q - pad[x, y - 1], pad[x, y + 1] - q),
                limit(q - before, after - q),
            ],
            axis=1,
        ).astype(BF16)
        contrib[b] = jnp.dot(moments, w[b], preferred_element_type=F32)

    def inner_plane(x, carry):
        load_weights(x - 1).wait()
        for y in range(2, 16):
            contribute(x, y)
        return carry

    lax.fori_loop(2, 8, inner_plane, 0)
    lane = lax.broadcasted_iota(jnp.int32, (128, 128), 1)
    sub = lax.broadcasted_iota(jnp.int32, (128, 128), 0)
    named = jnp.broadcast_to(numbers[0:1], (128, 128)).T == lane
    first = jnp.min(jnp.where(named, sub, 128), axis=0, keepdims=True)
    last = jnp.max(jnp.where(named, sub, -1), axis=0, keepdims=True)
    slotv[...] = jnp.concatenate([first, jnp.where(last > first, last, 128)] * 4, axis=0)
    fetch_slots = pltpu.make_async_copy(slotv, slots, slot_sem.at[0])
    fetch_slots.start()
    contrib[128] = jnp.zeros((16, 128), F32)
    received(pad.at[0:3, inner], HALO)

    @pl.when(gx == 0)
    def _():
        pad[0, 1:17] = jnp.zeros((16, 16, 128), F32)

    @pl.when(gx == 3)
    def _():
        pad[9, 1:17] = jnp.zeros((16, 16, 128), F32)

    @pl.when(gy == 0)
    def _():
        pad[1:9, 0] = jnp.zeros((8, 16, 128), F32)

    @pl.when(gy == 3)
    def _():
        pad[1:9, 17] = jnp.zeros((8, 16, 128), F32)

    def side_columns(x, carry):
        contribute(x, 1)
        contribute(x, 16)
        return carry

    lax.fori_loop(2, 8, side_columns, 0)
    load_weights(0).wait()
    load_weights(7).wait()

    def side_planes(side, carry):
        for y in range(1, 17):
            contribute(1 + side * 7, y)
        return carry

    lax.fori_loop(0, 2, side_planes, 0)
    fetch_slots.wait()
    pl.semaphore_wait(lines_sem, 15)

    for i, offset in enumerate(OFFSETS):
        device = at(*offset)
        to = device[0] * 32 + device[1] * 8 + device[2]
        for slot in range(2):
            held = contrib[jnp.clip(slots[slot, to], 0, 128)]
            if i == 127:
                recvbuf[i, slot] = held
            else:
                sendbuf[i, slot] = held
        if i < 127:
            remote(sendbuf.at[i], recvbuf.at[i], DELIVERY, device, i // STEPS).start()
        if i == 15:
            received(meta.at[0, 1:8], META_LINE)
            for k, (a, b) in enumerate(plane[1:]):
                remote(meta.at[0], meta.at[k + 1], META_PLANE, at(a, b, 0)).start()

    received(meta.at[1:16], META_PLANE)
    for i, (a, b, c) in enumerate(OFFSETS):
        row = meta[a * 4 + b, c]
        metat[0, i : i + 1, :] = row[0:1]
        metat[1, i : i + 1, :] = row[1:2]
    mine = metat[0] == me
    target = metat[1].astype(F32)
    lane = lane.astype(F32)
    first = jnp.min(jnp.where(mine, lane, 128.0), axis=1, keepdims=True)
    last = jnp.max(jnp.where(mine, lane, -1.0), axis=1, keepdims=True)
    target_0 = jnp.max(jnp.where(mine & (lane == first), target, -1.0), axis=1, keepdims=True)
    target_1 = jnp.max(jnp.where(mine & (lane == last) & (last > first), target, -1.0), axis=1, keepdims=True)
    hot_0 = jnp.where(target_0 == lane, 1.0, 0.0)
    hot_1 = jnp.where(target_1 == lane, 1.0, 0.0)
    for chunk in range(CHUNKS):
        rows = slice(chunk * STEPS, (chunk + 1) * STEPS)
        both = jnp.concatenate([hot_0[rows], hot_1[rows], hot_0[rows], hot_1[rows]], axis=0)
        lhs[chunk] = both.T.astype(BF16)

    for chunk in range(CHUNKS):
        start = chunk * STEPS
        received(recvbuf.at[start : min(start + STEPS, 127)], DELIVERY, chunk)
        for part in range(STEPS // 16):
            for slot in range(2):
                for half in range(2):
                    tile = recvbuf[pl.ds(start + part * 16, 16), slot, pl.ds(half * 8, 8), :]
                    tile = jnp.swapaxes(tile, 0, 1)
                    upper = tile.astype(BF16)
                    lower = (tile - upper.astype(F32)).astype(BF16)
                    row = slot * STEPS + part * 16
                    rhs[pl.ds(half * 8, 8), pl.ds(row, 16), :] = upper
                    rhs[pl.ds(half * 8, 8), pl.ds(2 * STEPS + row, 16), :] = lower
        for f in range(16):
            part_sum = jnp.dot(lhs[chunk], rhs[f], preferred_element_type=F32)
            fields[f] = part_sum if chunk == 0 else fields[f] + part_sum

    square = fields[4] * fields[4] + (fields[1] * fields[1] + fields[2] * fields[2] + fields[3] * fields[3])
    own_core = lax.rem(gz, 2)
    other_core = (gx, gy, gz + 1 - 2 * own_core)
    max1[0] = jnp.max(square.reshape(16, 8, 128), axis=0)
    remote(max1.at[0], max1.at[1], SPEED_CORE, other_core).start()

    def rim_send(src, dst, device):
        remote(src, dst, RIM, device).start()

    rim_send(fields.at[pl.ds(0, 4), pl.ds(112, 16)], xrecv.at[0], at(1, 0, 0))
    rim_send(fields.at[pl.ds(0, 4), pl.ds(0, 16)], xrecv.at[1], at(-1, 0, 0))
    for f in range(4):
        planes = fields[f].reshape(8, 16, 128)
        ysend[0, f] = planes[:, 0]
        ysend[1, f] = planes[:, 15]
    rim_send(ysend.at[1], yrecv.at[0], at(0, 1, 0))
    rim_send(ysend.at[0], yrecv.at[1], at(0, -1, 0))
    for dx in (1, -1):
        for dy in (1, -1):
            rim_send(ysend.at[(1 + dy) // 2], erecv.at[(1 - dx) // 2, (1 - dy) // 2], at(dx, dy, 0))

    def columns(x, carry):
        low, high = carry
        for f in range(4):
            l = (x + 1) * 4 + f
            rolled = pltpu.roll(fields[f, pl.ds(pl.multiple_of(x * 16, 16), 16), :], l, 1)
            low = jnp.where(lane16 == l, rolled, low)
            high = jnp.where(lane16 == l - 1, rolled, high)
        return low, high

    low, high = lax.fori_loop(0, 8, columns, (zeros, zeros))
    zcol[0] = low
    zcol[1] = pltpu.roll(high, 1, 1)
    for dx in (0, 1, -1):
        for dy in (0, 1, -1):
            rim_send(zcol.at[1], zcolr.at[0, 1 - dx, 1 - dy], at(dx, dy, 1))
            rim_send(zcol.at[0], zcolr.at[1, 1 - dx, 1 - dy], at(dx, dy, -1))

    received(max1.at[1:2], SPEED_CORE)
    max2[0] = jnp.max(jnp.maximum(max1[0], max1[1]), axis=0, keepdims=True)
    chips = [offset for offset in OFFSETS if offset[2] % 2 == 0]
    for k, offset in enumerate(chips[:63]):
        remote(max2.at[0], max2.at[k + 1], SPEED_CHIPS, at(*offset)).start()

    received(contrib.at[0:38], RIM)
    sub8 = lax.broadcasted_iota(jnp.int32, (8, 128), 0)
    no_xl, no_xh = gx == 0, gx == 3
    no_yl, no_yh = gy == 0, gy == 3

    def tail(above, below):
        above = jnp.where(no_yh, 0.0, above)
        below = jnp.where(no_yl, 0.0, below)
        return jnp.where(sub8 == 7, below, above)

    def row(ref, *index):
        return jnp.broadcast_to(ref[index], (8, 128))

    def padded(f, x):
        if 1 <= x <= 8:
            cells = fields[f, (x - 1) * 16 : x * 16]
            edge = slice(x - 1, x)
            return jnp.concatenate([cells, tail(row(yrecv, 1, f, edge), row(yrecv, 0, f, edge))], axis=0)
        side, none, edge = (0, no_xl, slice(7, 8)) if x == 0 else (1, no_xh, slice(0, 1))
        rows = tail(row(erecv, side, 1, f, edge), row(erecv, side, 0, f, edge))
        return jnp.where(none, 0.0, jnp.concatenate([xrecv[side, f], rows], axis=0))

    lane24 = lax.broadcasted_iota(jnp.int32, (24, 128), 1)

    def gathered(side, none):
        tiles = []
        for dx in range(3):
            tiles.append(
                jnp.concatenate(
                    [zcolr[side, dx, 1], tail(zcolr[side, dx, 2, 0:8], zcolr[side, dx, 0, 8:16])], axis=0
                )
            )
        below = jnp.where(no_xl, 0.0, pltpu.roll(tiles[0], 96, 1))
        above = jnp.where(no_xh, 0.0, pltpu.roll(tiles[2], 32, 1))
        whole = jnp.where(lane24 < 4, below, jnp.where(lane24 < 36, tiles[1], above))
        return jnp.where(none, 0.0, whole)

    z_low = gathered(0, gz == 0)
    z_high = gathered(1, gz == 7)

    def along_z(f, x):
        q = padded(f, x)
        l = x * 4 + f
        before = jnp.where(lane24 == 0, pltpu.roll(z_low, (128 - l) % 128, 1), pltpu.roll(q, 1, 1))
        after = jnp.where(lane24 == 127, pltpu.roll(z_high, 127 - l, 1), pltpu.roll(q, 127, 1))
        return before + 2.0 * q + after, after - before

    def smooth_y(v):
        return (pltpu.roll(v, 1, 0) + 2.0 * v + pltpu.roll(v, 23, 0))[0:16]

    def spread_y(v):
        return (pltpu.roll(v, 23, 0) - pltpu.roll(v, 1, 0))[0:16]

    def plane_terms(x):
        p_s, p_d = along_z(0, x)
        u_s, _ = along_z(1, x)
        v_s, _ = along_z(2, x)
        _, w_d = along_z(3, x)
        return (
            smooth_y(p_s), spread_y(p_s), smooth_y(p_d),
            smooth_y(u_s), spread_y(v_s) + smooth_y(w_d),
        )

    terms = [plane_terms(0), plane_terms(1)]
    for x in range(8):
        terms.append(plane_terms(x + 2))
        before, here, after = terms[x : x + 3]
        gradient = (
            after[0] - before[0],
            before[1] + 2.0 * here[1] + after[1],
            before[2] + 2.0 * here[2] + after[2],
        )
        divergence = after[3] - before[3] + (before[4] + 2.0 * here[4] + after[4])
        rim[3, x] = divergence * (1.0 / 32.0)
        for k in range(3):
            rim[k, x] = gradient[k] * (1.0 / 32.0)

    delivered(contrib.at[0:38], RIM)
    received(max2.at[1:64], SPEED_CHIPS)
    largest = jnp.max(jnp.max(max2[...], axis=0), axis=1, keepdims=True)
    step = 0.5 / jnp.sqrt(1.0 + 0.05 * largest)
    step = jnp.broadcast_to(step, (16, 128))

    def advance(x):
        rows = slice(x * 16, x * 16 + 16)
        divergence = rim[3, x]
        pressure = fields[0, rows]
        fields[4, rows] = fields[4, rows] - step * pressure * divergence
        fields[0, rows] = pressure - step * divergence
        for k in range(3):
            fields[1 + k, rows] = fields[1 + k, rows] - step * rim[k, x]

    for x in range(8):
        advance(x)
    delivered(zsend, HALO_Z)
    delivered(pad.at[0:3, inner], HALO)
    delivered(meta.at[0, 1:8], META_LINE)
    delivered(meta.at[1:16], META_PLANE)
    delivered(sendbuf.at[0:127], DELIVERY)
    delivered(max1.at[1:2], SPEED_CORE)
    delivered(max2.at[1:64], SPEED_CHIPS)


def on_device(old_state, remap_weights, new_owner, new_block):
    dma = pltpu.SemaphoreType.DMA
    hbm = pl.BlockSpec(memory_space=pltpu.HBM)
    vmem = pl.BlockSpec(memory_space=pltpu.VMEM)
    out = pl.pallas_call(
        kernel,
        out_shape=jax.ShapeDtypeStruct((16, 128, 128), F32),
        in_specs=[hbm, hbm, vmem],
        out_specs=vmem,
        scratch_shapes=[
            pltpu.VMEM((128, 512, 128), BF16),
            pltpu.VMEM((16, 8, 16, 128), F32),
            pltpu.VMEM((10, 18, 16, 128), F32),
            pltpu.VMEM((2, 16, 128), F32),
            pltpu.VMEM((2, 16, 128), F32),
            pltpu.VMEM((129, 16, 128), F32),
            pltpu.VMEM((128, 2, 16, 128), F32),
            pltpu.VMEM((128, 2, 16, 128), F32),
            pltpu.VMEM((16, 8, 2, 128), jnp.int32),
            pltpu.VMEM((2, 128, 128), jnp.int32),
            pltpu.VMEM((8, 128), jnp.int32),
            pltpu.SMEM((8, 128), jnp.int32),
            pltpu.VMEM((CHUNKS, 128, 128), BF16),
            pltpu.VMEM((16, 128, 128), BF16),
            pltpu.VMEM((4, 8, 16, 128), F32),
            pltpu.VMEM((2, 4, 16, 128), F32),
            pltpu.VMEM((2, 4, 8, 128), F32),
            pltpu.VMEM((2, 4, 8, 128), F32),
            pltpu.VMEM((2, 2, 4, 8, 128), F32),
            pltpu.VMEM((2, 16, 128), F32),
            pltpu.VMEM((2, 3, 3, 16, 128), F32),
            pltpu.VMEM((2, 8, 128), F32),
            pltpu.VMEM((64, 1, 128), F32),
            pltpu.SemaphoreType.REGULAR,
            dma((8,)), dma((1,)), dma((1,)), dma((8,)), dma((7 + CHUNKS,)),
        ],
        compiler_params=pltpu.CompilerParams(
            collective_id=0, has_side_effects=True, vmem_limit_bytes=52 * 2**20
        ),
        cost_estimate=pl.CostEstimate(flops=2 * 16 * 512 * 128 * 128, bytes_accessed=20 * 2**20, transcendentals=0),
    )(
        old_state,
        remap_weights.reshape(128, 512, 128),
        jnp.concatenate([new_owner.reshape(1, 128), new_block.reshape(1, 128)], axis=0),
    )
    return out.reshape(16, 8, 16, 128)


def solution(mesh):
    return jax.shard_map(
        on_device,
        mesh=mesh,
        in_specs=(
            P(None, "gx", "gy", "gz"),
            P(("gx", "gy", "gz"), None, None, None),
            P(("gx", "gy", "gz"), None),
            P(("gx", "gy", "gz")),
        ),
        out_specs=P(None, "gx", "gy", "gz"),
        check_vma=False,
    )
```

```python
import jax
import jax.numpy as jnp
import numpy as np
from jax import lax
from jax.experimental import pallas as pl
from jax.experimental.pallas import tpu as pltpu
from jax.sharding import PartitionSpec as P

MESH = pl.DeviceIdType.MESH
F32 = jnp.float32
BF16 = jnp.bfloat16
CHUNKS = 4
STEPS = 128 // CHUNKS
HALO_Z, HALO_X, HALO_Y, META_LINE, META_PLANE, RIM, SPEED_CORE, SPEED_CHIPS, DELIVERY = range(9)


def far_first():
    draws = np.random.RandomState(0).permutation(128)
    cells = [(int(t) // 32, int(t) // 8 % 4, int(t) % 8) for t in draws if t]
    cells.sort(key=lambda o: -(min(o[0], 4 - o[0]) + min(o[1], 4 - o[1]) + (min(o[2], 8 - o[2]) + 1) // 2))
    order = []
    for a, b, c in cells:
        for offset in ((a, b, c), (-a % 4, -b % 4, -c % 8)):
            if offset not in order:
                order.append(offset)
    return order + [(0, 0, 0)]


OFFSETS = far_first()


def limit(below, above):
    return jnp.maximum(jnp.minimum(below, above), 0.0) + jnp.minimum(jnp.maximum(below, above), 0.0)


def kernel(
    state, weights, numbers, fields,
    w, nat, pad, zsend, zrecv, contrib, sendbuf, recvbuf, meta, metat, slotv, slots, lhs, rhs, rim,
    xrecv, ysend, yrecv, erecv, zcol, zcolr, max1, max2,
    lines_sem, w_sem, in_sem, slot_sem, sent, got,
):
    gx, gy, gz = lax.axis_index("gx"), lax.axis_index("gy"), lax.axis_index("gz")
    me = (gx * 4 + gy) * 8 + gz

    def around(here, size):
        steps = [here]
        for step in range(1, size):
            there = here + step
            steps.append(jnp.where(there >= size, there - size, there))
        return steps

    xs, ys, zs = around(gx, 4), around(gy, 4), around(gz, 8)

    def at(a, b, c):
        return xs[a % 4], ys[b % 4], zs[c % 8]

    def remote(src, dst, group, device, part=0):
        return pltpu.make_async_remote_copy(
            src_ref=src, dst_ref=dst, send_sem=sent.at[group], recv_sem=got.at[group + part], device_id=device,
            device_id_type=MESH,
        )

    def received(ref, group, part=0):
        remote(ref, ref, group, at(0, 0, 1), part).wait_recv()

    def delivered(ref, group):
        remote(ref, ref, group, at(0, 0, 1)).wait_send()

    load_state = pltpu.make_async_copy(state, nat, in_sem.at[0])
    load_state.start()

    def load_weights(x):
        return pltpu.make_async_copy(weights.at[pl.ds(x * 16, 16)], w.at[pl.ds(x * 16, 16)], w_sem.at[x])

    barrier = pltpu.get_barrier_semaphore()


    def greet(semaphore, device):
        pl.semaphore_signal(semaphore, inc=1, device_id=device, device_id_type=MESH)

    plane = [(a, b) for a in range(4) for b in range(4)]
    for a, b in plane[1:]:
        greet(barrier, at(a, b, 0))
    for c in range(1, 8):
        greet(barrier, at(0, 0, c))

    load_state.wait()
    for x in (1, 2, 3):
        load_weights(x).start()
    lane16 = lax.broadcasted_iota(jnp.int32, (16, 128), 1)

    def to_blocks(x, carry):
        low, high = carry
        for part in range(2):
            for half in range(2):
                tile = nat[pl.ds(half * 8, 8), x, pl.ds(part * 8, 8), :]
                pad[x + 1, pl.ds(1 + part * 8, 8), pl.ds(half * 8, 8), :] = jnp.swapaxes(tile, 0, 1)
        for y in range(16):
            b = x * 16 + y
            rolled = pltpu.roll(pad[x + 1, y + 1], b, 1)
            low = jnp.where(lane16 == b, rolled, low)
            high = jnp.where(lane16 == (b + 127) % 128, rolled, high)
        return low, high

    zeros = jnp.zeros((16, 128), F32)
    low, high = lax.fori_loop(0, 8, to_blocks, (zeros, zeros))
    zsend[0] = low
    zsend[1] = pltpu.roll(high, 1, 1)
    pl.semaphore_wait(barrier, 22)

    inner = pl.ds(1, 16)
    cells = pl.ds(1, 8)
    remote(zsend.at[1], zrecv.at[0], HALO_Z, at(0, 0, 1)).start()
    remote(zsend.at[0], zrecv.at[1], HALO_Z, at(0, 0, -1)).start()
    remote(pad.at[8, inner], pad.at[0, inner], HALO_X, at(1, 0, 0)).start()
    remote(pad.at[1, inner], pad.at[9, inner], HALO_X, at(-1, 0, 0)).start()
    remote(pad.at[cells, 16], pad.at[cells, 0], HALO_Y, at(0, 1, 0)).start()
    remote(pad.at[cells, 1], pad.at[cells, 17], HALO_Y, at(0, -1, 0)).start()
    for x in (4, 5, 6, 0, 7):
        load_weights(x).start()

    for a, b in plane[1:]:
        greet(lines_sem, at(a, b, 0))
    meta[0, 0] = numbers[...]
    for c in range(1, 8):
        remote(meta.at[0, 0], meta.at[0, c], META_LINE, at(0, 0, c)).start()

    received(zrecv, HALO_Z)
    z_low = jnp.where(gz == 0, 0.0, zrecv[0])
    z_high = jnp.where(gz == 7, 0.0, zrecv[1])

    def contribute(x, y):
        b = (x - 1) * 16 + (y - 1)
        q = pad[x, y]
        before = jnp.where(lane16 == 0, pltpu.roll(z_low, (128 - b) % 128, 1), pltpu.roll(q, 1, 1))
        after = jnp.where(lane16 == 127, pltpu.roll(z_high, 127 - b, 1), pltpu.roll(q, 127, 1))
        moments = jnp.concatenate(
            [
                q,
                limit(q - pad[x - 1, y], pad[x + 1, y] - q),
                limit(q - pad[x, y - 1], pad[x, y + 1] - q),
                limit(q - before, after - q),
            ],
            axis=1,
        ).astype(BF16)
        contrib[b] = jnp.dot(moments, w[b], preferred_element_type=F32)

    def inner_plane(x, carry):
        load_weights(x - 1).wait()
        for y in range(2, 16):
            contribute(x, y)
        return carry

    lax.fori_loop(2, 8, inner_plane, 0)
    lane = lax.broadcasted_iota(jnp.int32, (128, 128), 1)
    sub = lax.broadcasted_iota(jnp.int32, (128, 128), 0)
    named = jnp.broadcast_to(numbers[0:1], (128, 128)).T == lane
    first = jnp.min(jnp.where(named, sub, 128), axis=0, keepdims=True)
    last = jnp.max(jnp.where(named, sub, -1), axis=0, keepdims=True)
    slotv[...] = jnp.concatenate([first, jnp.where(last > first, last, 128)] * 4, axis=0)
    fetch_slots = pltpu.make_async_copy(slotv, slots, slot_sem.at[0])
    fetch_slots.start()
    contrib[128] = jnp.zeros((16, 128), F32)
    received(pad.at[0, inner], HALO_Y)

    @pl.when(gy == 0)
    def _():
        pad[1:9, 0] = jnp.zeros((8, 16, 128), F32)

    @pl.when(gy == 3)
    def _():
        pad[1:9, 17] = jnp.zeros((8, 16, 128), F32)

    def side_columns(x, carry):
        contribute(x, 1)
        contribute(x, 16)
        return carry

    lax.fori_loop(2, 8, side_columns, 0)
    received(pad.at[0:2, inner], HALO_X)

    @pl.when(gx == 0)
    def _():
        pad[0, 1:17] = jnp.zeros((16, 16, 128), F32)

    @pl.when(gx == 3)
    def _():
        pad[9, 1:17] = jnp.zeros((16, 16, 128), F32)

    load_weights(0).wait()
    load_weights(7).wait()

    def side_planes(side, carry):
        for y in range(1, 17):
            contribute(1 + side * 7, y)
        return carry

    lax.fori_loop(0, 2, side_planes, 0)
    fetch_slots.wait()
    pl.semaphore_wait(lines_sem, 15)

    for i, offset in enumerate(OFFSETS):
        device = at(*offset)
        to = device[0] * 32 + device[1] * 8 + device[2]
        for slot in range(2):
            held = contrib[jnp.clip(slots[slot, to], 0, 128)]
            if i == 127:
                recvbuf[i, slot] = held
            else:
                sendbuf[i, slot] = held
        if i < 127:
            remote(sendbuf.at[i], recvbuf.at[i], DELIVERY, device, i // STEPS).start()
        if i == 15:
            received(meta.at[0, 1:8], META_LINE)
            for k, (a, b) in enumerate(plane[1:]):
                remote(meta.at[0], meta.at[k + 1], META_PLANE, at(a, b, 0)).start()

    received(meta.at[1:16], META_PLANE)
    for i, (a, b, c) in enumerate(OFFSETS):
        row = meta[a * 4 + b, c]
        metat[0, i : i + 1, :] = row[0:1]
        metat[1, i : i + 1, :] = row[1:2]
    mine = metat[0] == me
    target = metat[1].astype(F32)
    lane = lane.astype(F32)
    first = jnp.min(jnp.where(mine, lane, 128.0), axis=1, keepdims=True)
    last = jnp.max(jnp.where(mine, lane, -1.0), axis=1, keepdims=True)
    target_0 = jnp.max(jnp.where(mine & (lane == first), target, -1.0), axis=1, keepdims=True)
    target_1 = jnp.max(jnp.where(mine & (lane == last) & (last > first), target, -1.0), axis=1, keepdims=True)
    hot_0 = jnp.where(target_0 == lane, 1.0, 0.0)
    hot_1 = jnp.where(target_1 == lane, 1.0, 0.0)
    for chunk in range(CHUNKS):
        rows = slice(chunk * STEPS, (chunk + 1) * STEPS)
        both = jnp.concatenate([hot_0[rows], hot_1[rows], hot_0[rows], hot_1[rows]], axis=0)
        lhs[chunk] = both.T.astype(BF16)

    for chunk in range(CHUNKS):
        start = chunk * STEPS
        received(recvbuf.at[start : min(start + STEPS, 127)], DELIVERY, chunk)
        for part in range(STEPS // 16):
            for slot in range(2):
                for half in range(2):
                    tile = recvbuf[pl.ds(start + part * 16, 16), slot, pl.ds(half * 8, 8), :]
                    tile = jnp.swapaxes(tile, 0, 1)
                    upper = tile.astype(BF16)
                    lower = (tile - upper.astype(F32)).astype(BF16)
                    row = slot * STEPS + part * 16
                    rhs[pl.ds(half * 8, 8), pl.ds(row, 16), :] = upper
                    rhs[pl.ds(half * 8, 8), pl.ds(2 * STEPS + row, 16), :] = lower
        for f in range(16):
            part_sum = jnp.dot(lhs[chunk], rhs[f], preferred_element_type=F32)
            fields[f] = part_sum if chunk == 0 else fields[f] + part_sum

    square = fields[4] * fields[4] + (fields[1] * fields[1] + fields[2] * fields[2] + fields[3] * fields[3])
    own_core = lax.rem(gz, 2)
    other_core = (gx, gy, gz + 1 - 2 * own_core)
    max1[0] = jnp.max(square.reshape(16, 8, 128), axis=0)
    remote(max1.at[0], max1.at[1], SPEED_CORE, other_core).start()

    def rim_send(src, dst, device):
        remote(src, dst, RIM, device).start()

    rim_send(fields.at[pl.ds(0, 4), pl.ds(112, 16)], xrecv.at[0], at(1, 0, 0))
    rim_send(fields.at[pl.ds(0, 4), pl.ds(0, 16)], xrecv.at[1], at(-1, 0, 0))
    for f in range(4):
        planes = fields[f].reshape(8, 16, 128)
        ysend[0, f] = planes[:, 0]
        ysend[1, f] = planes[:, 15]
    rim_send(ysend.at[1], yrecv.at[0], at(0, 1, 0))
    rim_send(ysend.at[0], yrecv.at[1], at(0, -1, 0))
    for dx in (1, -1):
        for dy in (1, -1):
            rim_send(ysend.at[(1 + dy) // 2], erecv.at[(1 - dx) // 2, (1 - dy) // 2], at(dx, dy, 0))

    def columns(x, carry):
        low, high = carry
        for f in range(4):
            l = (x + 1) * 4 + f
            rolled = pltpu.roll(fields[f, pl.ds(pl.multiple_of(x * 16, 16), 16), :], l, 1)
            low = jnp.where(lane16 == l, rolled, low)
            high = jnp.where(lane16 == l - 1, rolled, high)
        return low, high

    low, high = lax.fori_loop(0, 8, columns, (zeros, zeros))
    zcol[0] = low
    zcol[1] = pltpu.roll(high, 1, 1)
    for dx in (0, 1, -1):
        for dy in (0, 1, -1):
            rim_send(zcol.at[1], zcolr.at[0, 1 - dx, 1 - dy], at(dx, dy, 1))
            rim_send(zcol.at[0], zcolr.at[1, 1 - dx, 1 - dy], at(dx, dy, -1))

    received(max1.at[1:2], SPEED_CORE)
    max2[0] = jnp.max(jnp.maximum(max1[0], max1[1]), axis=0, keepdims=True)
    chips = [offset for offset in OFFSETS if offset[2] % 2 == 0]
    for k, offset in enumerate(chips[:63]):
        remote(max2.at[0], max2.at[k + 1], SPEED_CHIPS, at(*offset)).start()

    received(contrib.at[0:38], RIM)
    sub8 = lax.broadcasted_iota(jnp.int32, (8, 128), 0)
    no_xl, no_xh = gx == 0, gx == 3
    no_yl, no_yh = gy == 0, gy == 3

    def tail(above, below):
        above = jnp.where(no_yh, 0.0, above)
        below = jnp.where(no_yl, 0.0, below)
        return jnp.where(sub8 == 7, below, above)

    def row(ref, *index):
        return jnp.broadcast_to(ref[index], (8, 128))

    def padded(f, x):
        if 1 <= x <= 8:
            cells = fields[f, (x - 1) * 16 : x * 16]
            edge = slice(x - 1, x)
            return jnp.concatenate([cells, tail(row(yrecv, 1, f, edge), row(yrecv, 0, f, edge))], axis=0)
        side, none, edge = (0, no_xl, slice(7, 8)) if x == 0 else (1, no_xh, slice(0, 1))
        rows = tail(row(erecv, side, 1, f, edge), row(erecv, side, 0, f, edge))
        return jnp.where(none, 0.0, jnp.concatenate([xrecv[side, f], rows], axis=0))

    lane24 = lax.broadcasted_iota(jnp.int32, (24, 128), 1)

    def gathered(side, none):
        tiles = []
        for dx in range(3):
            tiles.append(
                jnp.concatenate(
                    [zcolr[side, dx, 1], tail(zcolr[side, dx, 2, 0:8], zcolr[side, dx, 0, 8:16])], axis=0
                )
            )
        below = jnp.where(no_xl, 0.0, pltpu.roll(tiles[0], 96, 1))
        above = jnp.where(no_xh, 0.0, pltpu.roll(tiles[2], 32, 1))
        whole = jnp.where(lane24 < 4, below, jnp.where(lane24 < 36, tiles[1], above))
        return jnp.where(none, 0.0, whole)

    z_low = gathered(0, gz == 0)
    z_high = gathered(1, gz == 7)

    def along_z(f, x):
        q = padded(f, x)
        l = x * 4 + f
        before = jnp.where(lane24 == 0, pltpu.roll(z_low, (128 - l) % 128, 1), pltpu.roll(q, 1, 1))
        after = jnp.where(lane24 == 127, pltpu.roll(z_high, 127 - l, 1), pltpu.roll(q, 127, 1))
        return before + 2.0 * q + after, after - before

    def smooth_y(v):
        return (pltpu.roll(v, 1, 0) + 2.0 * v + pltpu.roll(v, 23, 0))[0:16]

    def spread_y(v):
        return (pltpu.roll(v, 23, 0) - pltpu.roll(v, 1, 0))[0:16]

    def plane_terms(x):
        p_s, p_d = along_z(0, x)
        u_s, _ = along_z(1, x)
        v_s, _ = along_z(2, x)
        _, w_d = along_z(3, x)
        return (
            smooth_y(p_s), spread_y(p_s), smooth_y(p_d),
            smooth_y(u_s), spread_y(v_s) + smooth_y(w_d),
        )

    terms = [plane_terms(0), plane_terms(1)]
    for x in range(8):
        terms.append(plane_terms(x + 2))
        before, here, after = terms[x : x + 3]
        gradient = (
            after[0] - before[0],
            before[1] + 2.0 * here[1] + after[1],
            before[2] + 2.0 * here[2] + after[2],
        )
        divergence = after[3] - before[3] + (before[4] + 2.0 * here[4] + after[4])
        rim[3, x] = divergence * (1.0 / 32.0)
        for k in range(3):
            rim[k, x] = gradient[k] * (1.0 / 32.0)

    delivered(contrib.at[0:38], RIM)
    received(max2.at[1:64], SPEED_CHIPS)
    largest = jnp.max(jnp.max(max2[...], axis=0), axis=1, keepdims=True)
    step = 0.5 / jnp.sqrt(1.0 + 0.05 * largest)
    step = jnp.broadcast_to(step, (16, 128))

    def advance(x):
        rows = slice(x * 16, x * 16 + 16)
        divergence = rim[3, x]
        pressure = fields[0, rows]
        fields[4, rows] = fields[4, rows] - step * pressure * divergence
        fields[0, rows] = pressure - step * divergence
        for k in range(3):
            fields[1 + k, rows] = fields[1 + k, rows] - step * rim[k, x]

    for x in range(8):
        advance(x)
    delivered(zsend, HALO_Z)
    delivered(pad.at[0:2, inner], HALO_X)
    delivered(pad.at[0, inner], HALO_Y)
    delivered(meta.at[0, 1:8], META_LINE)
    delivered(meta.at[1:16], META_PLANE)
    delivered(sendbuf.at[0:127], DELIVERY)
    delivered(max1.at[1:2], SPEED_CORE)
    delivered(max2.at[1:64], SPEED_CHIPS)


def on_device(old_state, remap_weights, new_owner, new_block):
    dma = pltpu.SemaphoreType.DMA
    hbm = pl.BlockSpec(memory_space=pltpu.HBM)
    vmem = pl.BlockSpec(memory_space=pltpu.VMEM)
    out = pl.pallas_call(
        kernel,
        out_shape=jax.ShapeDtypeStruct((16, 128, 128), F32),
        in_specs=[hbm, hbm, vmem],
        out_specs=vmem,
        scratch_shapes=[
            pltpu.VMEM((128, 512, 128), BF16),
            pltpu.VMEM((16, 8, 16, 128), F32),
            pltpu.VMEM((10, 18, 16, 128), F32),
            pltpu.VMEM((2, 16, 128), F32),
            pltpu.VMEM((2, 16, 128), F32),
            pltpu.VMEM((129, 16, 128), F32),
            pltpu.VMEM((128, 2, 16, 128), F32),
            pltpu.VMEM((128, 2, 16, 128), F32),
            pltpu.VMEM((16, 8, 2, 128), jnp.int32),
            pltpu.VMEM((2, 128, 128), jnp.int32),
            pltpu.VMEM((8, 128), jnp.int32),
            pltpu.SMEM((8, 128), jnp.int32),
            pltpu.VMEM((CHUNKS, 128, 128), BF16),
            pltpu.VMEM((16, 128, 128), BF16),
            pltpu.VMEM((4, 8, 16, 128), F32),
            pltpu.VMEM((2, 4, 16, 128), F32),
            pltpu.VMEM((2, 4, 8, 128), F32),
            pltpu.VMEM((2, 4, 8, 128), F32),
            pltpu.VMEM((2, 2, 4, 8, 128), F32),
            pltpu.VMEM((2, 16, 128), F32),
            pltpu.VMEM((2, 3, 3, 16, 128), F32),
            pltpu.VMEM((2, 8, 128), F32),
            pltpu.VMEM((64, 1, 128), F32),
            pltpu.SemaphoreType.REGULAR,
            dma((8,)), dma((1,)), dma((1,)), dma((9,)), dma((8 + CHUNKS,)),
        ],
        compiler_params=pltpu.CompilerParams(
            collective_id=0, has_side_effects=True, vmem_limit_bytes=52 * 2**20
        ),
        cost_estimate=pl.CostEstimate(flops=2 * 16 * 512 * 128 * 128, bytes_accessed=20 * 2**20, transcendentals=0),
    )(
        old_state,
        remap_weights.reshape(128, 512, 128),
        jnp.concatenate([new_owner.reshape(1, 128), new_block.reshape(1, 128)], axis=0),
    )
    return out.reshape(16, 8, 16, 128)


def solution(mesh):
    return jax.shard_map(
        on_device,
        mesh=mesh,
        in_specs=(
            P(None, "gx", "gy", "gz"),
            P(("gx", "gy", "gz"), None, None, None),
            P(("gx", "gy", "gz"), None),
            P(("gx", "gy", "gz")),
        ),
        out_specs=P(None, "gx", "gy", "gz"),
        check_vma=False,
    )
```

```python
import jax
import jax.numpy as jnp
import numpy as np
from jax import lax
from jax.experimental import pallas as pl
from jax.experimental.pallas import tpu as pltpu
from jax.sharding import PartitionSpec as P

MESH = pl.DeviceIdType.MESH
F32 = jnp.float32
BF16 = jnp.bfloat16
CHUNKS = 4
STEPS = 128 // CHUNKS
HALO_Z, HALO_X, HALO_Y, META_LINE, META_PLANE, RIM, SPEED_CORE, SPEED_CHIPS, DELIVERY = range(9)


def far_first():
    draws = np.random.RandomState(0).permutation(128)
    cells = [(int(t) // 32, int(t) // 8 % 4, int(t) % 8) for t in draws if t]
    cells.sort(key=lambda o: -(min(o[0], 4 - o[0]) + min(o[1], 4 - o[1]) + (min(o[2], 8 - o[2]) + 1) // 2))
    order = []
    for a, b, c in cells:
        for offset in ((a, b, c), (-a % 4, -b % 4, -c % 8)):
            if offset not in order:
                order.append(offset)
    return order + [(0, 0, 0)]


OFFSETS = far_first()


def limit(below, above):
    return jnp.maximum(jnp.minimum(below, above), 0.0) + jnp.minimum(jnp.maximum(below, above), 0.0)


def kernel(
    state, weights, numbers, fields,
    w, nat, pad, zsend, zrecv, contrib, sendbuf, recvbuf, meta, metat, slotv, slots, lhs, rhs, rim,
    xrecv, ysend, yrecv, erecv, zcol, zcolr, max1, max2,
    lines_sem, w_sem, in_sem, slot_sem, sent, got,
):
    gx, gy, gz = lax.axis_index("gx"), lax.axis_index("gy"), lax.axis_index("gz")
    me = (gx * 4 + gy) * 8 + gz

    def around(here, size):
        steps = [here]
        for step in range(1, size):
            there = here + step
            steps.append(jnp.where(there >= size, there - size, there))
        return steps

    xs, ys, zs = around(gx, 4), around(gy, 4), around(gz, 8)

    def at(a, b, c):
        return xs[a % 4], ys[b % 4], zs[c % 8]

    def remote(src, dst, group, device, part=0):
        return pltpu.make_async_remote_copy(
            src_ref=src, dst_ref=dst, send_sem=sent.at[group], recv_sem=got.at[group + part], device_id=device,
            device_id_type=MESH,
        )

    def received(ref, group, part=0):
        remote(ref, ref, group, at(0, 0, 1), part).wait_recv()

    def delivered(ref, group):
        remote(ref, ref, group, at(0, 0, 1)).wait_send()

    load_state = pltpu.make_async_copy(state, nat, in_sem.at[0])
    load_state.start()

    def load_weights(x):
        return pltpu.make_async_copy(weights.at[pl.ds(x * 16, 16)], w.at[pl.ds(x * 16, 16)], w_sem.at[x])

    barrier = pltpu.get_barrier_semaphore()


    def greet(semaphore, device):
        pl.semaphore_signal(semaphore, inc=1, device_id=device, device_id_type=MESH)

    plane = [(a, b) for a in range(4) for b in range(4)]
    for a, b in plane[1:]:
        greet(barrier, at(a, b, 0))
    for c in range(1, 8):
        greet(barrier, at(0, 0, c))

    load_state.wait()
    for x in (1, 2, 3):
        load_weights(x).start()
    lane16 = lax.broadcasted_iota(jnp.int32, (16, 128), 1)

    def to_blocks(x, carry):
        low, high = carry
        for part in range(2):
            for half in range(2):
                tile = nat[pl.ds(half * 8, 8), x, pl.ds(part * 8, 8), :]
                pad[x + 1, pl.ds(1 + part * 8, 8), pl.ds(half * 8, 8), :] = jnp.swapaxes(tile, 0, 1)
        for y in range(16):
            b = x * 16 + y
            rolled = pltpu.roll(pad[x + 1, y + 1], b, 1)
            low = jnp.where(lane16 == b, rolled, low)
            high = jnp.where(lane16 == (b + 127) % 128, rolled, high)
        return low, high

    zeros = jnp.zeros((16, 128), F32)
    low, high = lax.fori_loop(0, 8, to_blocks, (zeros, zeros))
    zsend[0] = low
    zsend[1] = pltpu.roll(high, 1, 1)
    pl.semaphore_wait(barrier, 22)

    inner = pl.ds(1, 16)
    cells = pl.ds(1, 8)
    remote(zsend.at[1], zrecv.at[0], HALO_Z, at(0, 0, 1)).start()
    remote(zsend.at[0], zrecv.at[1], HALO_Z, at(0, 0, -1)).start()
    remote(pad.at[8, inner], pad.at[0, inner], HALO_X, at(1, 0, 0)).start()
    remote(pad.at[1, inner], pad.at[9, inner], HALO_X, at(-1, 0, 0)).start()
    remote(pad.at[cells, 16], pad.at[cells, 0], HALO_Y, at(0, 1, 0)).start()
    remote(pad.at[cells, 1], pad.at[cells, 17], HALO_Y, at(0, -1, 0)).start()
    for x in (4, 5, 6, 0, 7):
        load_weights(x).start()

    for a, b in plane[1:]:
        greet(lines_sem, at(a, b, 0))
    meta[0, 0] = numbers[...]
    for c in range(1, 8):
        remote(meta.at[0, 0], meta.at[0, c], META_LINE, at(0, 0, c)).start()

    received(zrecv, HALO_Z)
    z_low = jnp.where(gz == 0, 0.0, zrecv[0])
    z_high = jnp.where(gz == 7, 0.0, zrecv[1])

    def contribute(x, y):
        b = (x - 1) * 16 + (y - 1)
        q = pad[x, y]
        before = jnp.where(lane16 == 0, pltpu.roll(z_low, (128 - b) % 128, 1), pltpu.roll(q, 1, 1))
        after = jnp.where(lane16 == 127, pltpu.roll(z_high, 127 - b, 1), pltpu.roll(q, 127, 1))
        moments = jnp.concatenate(
            [
                q,
                limit(q - pad[x - 1, y], pad[x + 1, y] - q),
                limit(q - pad[x, y - 1], pad[x, y + 1] - q),
                limit(q - before, after - q),
            ],
            axis=1,
        ).astype(BF16)
        contrib[b] = jnp.dot(moments, w[b], preferred_element_type=F32)

    def inner_plane(x, carry):
        load_weights(x - 1).wait()
        for y in range(2, 16):
            contribute(x, y)
        return carry

    lax.fori_loop(2, 8, inner_plane, 0)
    lane = lax.broadcasted_iota(jnp.int32, (128, 128), 1)
    sub = lax.broadcasted_iota(jnp.int32, (128, 128), 0)
    named = jnp.broadcast_to(numbers[0:1], (128, 128)).T == lane
    first = jnp.min(jnp.where(named, sub, 128), axis=0, keepdims=True)
    last = jnp.max(jnp.where(named, sub, -1), axis=0, keepdims=True)
    slotv[...] = jnp.concatenate([first, jnp.where(last > first, last, 128)] * 4, axis=0)
    fetch_slots = pltpu.make_async_copy(slotv, slots, slot_sem.at[0])
    fetch_slots.start()
    contrib[128] = jnp.zeros((16, 128), F32)
    received(pad.at[0, inner], HALO_Y)

    @pl.when(gy == 0)
    def _():
        pad[1:9, 0] = jnp.zeros((8, 16, 128), F32)

    @pl.when(gy == 3)
    def _():
        pad[1:9, 17] = jnp.zeros((8, 16, 128), F32)

    def side_columns(x, carry):
        contribute(x, 1)
        contribute(x, 16)
        return carry

    lax.fori_loop(2, 8, side_columns, 0)
    received(pad.at[0:2, inner], HALO_X)

    @pl.when(gx == 0)
    def _():
        pad[0, 1:17] = jnp.zeros((16, 16, 128), F32)

    @pl.when(gx == 3)
    def _():
        pad[9, 1:17] = jnp.zeros((16, 16, 128), F32)

    load_weights(0).wait()
    load_weights(7).wait()

    def side_planes(side, carry):
        for y in range(1, 17):
            contribute(1 + side * 7, y)
        return carry

    lax.fori_loop(0, 2, side_planes, 0)
    fetch_slots.wait()
    pl.semaphore_wait(lines_sem, 15)

    for i, offset in enumerate(OFFSETS):
        device = at(*offset)
        to = device[0] * 32 + device[1] * 8 + device[2]
        for slot in range(2):
            held = contrib[jnp.clip(slots[slot, to], 0, 128)]
            if i == 127:
                recvbuf[i, slot] = held
            else:
                sendbuf[i, slot] = held
        if i < 127:
            remote(sendbuf.at[i], recvbuf.at[i], DELIVERY, device, i // STEPS).start()
        if i == 15:
            received(meta.at[0, 1:8], META_LINE)
            for k, (a, b) in enumerate(plane[1:]):
                remote(meta.at[0], meta.at[k + 1], META_PLANE, at(a, b, 0)).start()

    received(meta.at[1:16], META_PLANE)
    for i, (a, b, c) in enumerate(OFFSETS):
        row = meta[a * 4 + b, c]
        metat[0, i : i + 1, :] = row[0:1]
        metat[1, i : i + 1, :] = row[1:2]
    mine = metat[0] == me
    target = metat[1].astype(F32)
    lane = lane.astype(F32)
    first = jnp.min(jnp.where(mine, lane, 128.0), axis=1, keepdims=True)
    last = jnp.max(jnp.where(mine, lane, -1.0), axis=1, keepdims=True)
    target_0 = jnp.max(jnp.where(mine & (lane == first), target, -1.0), axis=1, keepdims=True)
    target_1 = jnp.max(jnp.where(mine & (lane == last) & (last > first), target, -1.0), axis=1, keepdims=True)
    hot_0 = jnp.where(target_0 == lane, 1.0, 0.0)
    hot_1 = jnp.where(target_1 == lane, 1.0, 0.0)
    for chunk in range(CHUNKS):
        rows = slice(chunk * STEPS, (chunk + 1) * STEPS)
        both = jnp.concatenate([hot_0[rows], hot_1[rows], hot_0[rows], hot_1[rows]], axis=0)
        lhs[chunk] = both.T.astype(BF16)

    def arrange(chunk, half):
        for part in range(STEPS // 16):
            for slot in range(2):
                tile = recvbuf[pl.ds(chunk * STEPS + part * 16, 16), slot, pl.ds(half * 8, 8), :]
                tile = jnp.swapaxes(tile, 0, 1)
                upper = tile.astype(BF16)
                lower = (tile - upper.astype(F32)).astype(BF16)
                row = slot * STEPS + part * 16
                rhs[pl.ds(half * 8, 8), pl.ds(row, 16), :] = upper
                rhs[pl.ds(half * 8, 8), pl.ds(2 * STEPS + row, 16), :] = lower

    def accumulate(chunk, which):
        for f in which:
            part_sum = jnp.dot(lhs[chunk], rhs[f], preferred_element_type=F32)
            fields[f] = part_sum if chunk == 0 else fields[f] + part_sum

    final = CHUNKS - 1
    for chunk in range(CHUNKS):
        start = chunk * STEPS
        received(recvbuf.at[start : min(start + STEPS, 127)], DELIVERY, chunk)
        arrange(chunk, 0)
        if chunk < final:
            arrange(chunk, 1)
            accumulate(chunk, range(16))
        else:
            accumulate(chunk, range(5))

    square = fields[4] * fields[4] + (fields[1] * fields[1] + fields[2] * fields[2] + fields[3] * fields[3])
    own_core = lax.rem(gz, 2)
    other_core = (gx, gy, gz + 1 - 2 * own_core)
    max1[0] = jnp.max(square.reshape(16, 8, 128), axis=0)
    remote(max1.at[0], max1.at[1], SPEED_CORE, other_core).start()

    def rim_send(src, dst, device):
        remote(src, dst, RIM, device).start()

    rim_send(fields.at[pl.ds(0, 4), pl.ds(112, 16)], xrecv.at[0], at(1, 0, 0))
    rim_send(fields.at[pl.ds(0, 4), pl.ds(0, 16)], xrecv.at[1], at(-1, 0, 0))
    for f in range(4):
        planes = fields[f].reshape(8, 16, 128)
        ysend[0, f] = planes[:, 0]
        ysend[1, f] = planes[:, 15]
    rim_send(ysend.at[1], yrecv.at[0], at(0, 1, 0))
    rim_send(ysend.at[0], yrecv.at[1], at(0, -1, 0))
    for dx in (1, -1):
        for dy in (1, -1):
            rim_send(ysend.at[(1 + dy) // 2], erecv.at[(1 - dx) // 2, (1 - dy) // 2], at(dx, dy, 0))

    def columns(x, carry):
        low, high = carry
        for f in range(4):
            l = (x + 1) * 4 + f
            rolled = pltpu.roll(fields[f, pl.ds(pl.multiple_of(x * 16, 16), 16), :], l, 1)
            low = jnp.where(lane16 == l, rolled, low)
            high = jnp.where(lane16 == l - 1, rolled, high)
        return low, high

    low, high = lax.fori_loop(0, 8, columns, (zeros, zeros))
    zcol[0] = low
    zcol[1] = pltpu.roll(high, 1, 1)
    for dx in (0, 1, -1):
        for dy in (0, 1, -1):
            rim_send(zcol.at[1], zcolr.at[0, 1 - dx, 1 - dy], at(dx, dy, 1))
            rim_send(zcol.at[0], zcolr.at[1, 1 - dx, 1 - dy], at(dx, dy, -1))

    received(max1.at[1:2], SPEED_CORE)
    max2[0] = jnp.max(jnp.maximum(max1[0], max1[1]), axis=0, keepdims=True)
    chips = [offset for offset in OFFSETS if offset[2] % 2 == 0]
    for k, offset in enumerate(chips[:63]):
        remote(max2.at[0], max2.at[k + 1], SPEED_CHIPS, at(*offset)).start()

    arrange(final, 1)
    accumulate(final, range(5, 16))

    received(contrib.at[0:38], RIM)
    sub8 = lax.broadcasted_iota(jnp.int32, (8, 128), 0)
    no_xl, no_xh = gx == 0, gx == 3
    no_yl, no_yh = gy == 0, gy == 3

    def tail(above, below):
        above = jnp.where(no_yh, 0.0, above)
        below = jnp.where(no_yl, 0.0, below)
        return jnp.where(sub8 == 7, below, above)

    def row(ref, *index):
        return jnp.broadcast_to(ref[index], (8, 128))

    def padded(f, x):
        if 1 <= x <= 8:
            cells = fields[f, (x - 1) * 16 : x * 16]
            edge = slice(x - 1, x)
            return jnp.concatenate([cells, tail(row(yrecv, 1, f, edge), row(yrecv, 0, f, edge))], axis=0)
        side, none, edge = (0, no_xl, slice(7, 8)) if x == 0 else (1, no_xh, slice(0, 1))
        rows = tail(row(erecv, side, 1, f, edge), row(erecv, side, 0, f, edge))
        return jnp.where(none, 0.0, jnp.concatenate([xrecv[side, f], rows], axis=0))

    lane24 = lax.broadcasted_iota(jnp.int32, (24, 128), 1)

    def gathered(side, none):
        tiles = []
        for dx in range(3):
            tiles.append(
                jnp.concatenate(
                    [zcolr[side, dx, 1], tail(zcolr[side, dx, 2, 0:8], zcolr[side, dx, 0, 8:16])], axis=0
                )
            )
        below = jnp.where(no_xl, 0.0, pltpu.roll(tiles[0], 96, 1))
        above = jnp.where(no_xh, 0.0, pltpu.roll(tiles[2], 32, 1))
        whole = jnp.where(lane24 < 4, below, jnp.where(lane24 < 36, tiles[1], above))
        return jnp.where(none, 0.0, whole)

    z_low = gathered(0, gz == 0)
    z_high = gathered(1, gz == 7)

    def along_z(f, x):
        q = padded(f, x)
        l = x * 4 + f
        before = jnp.where(lane24 == 0, pltpu.roll(z_low, (128 - l) % 128, 1), pltpu.roll(q, 1, 1))
        after = jnp.where(lane24 == 127, pltpu.roll(z_high, 127 - l, 1), pltpu.roll(q, 127, 1))
        return before + 2.0 * q + after, after - before

    def smooth_y(v):
        return (pltpu.roll(v, 1, 0) + 2.0 * v + pltpu.roll(v, 23, 0))[0:16]

    def spread_y(v):
        return (pltpu.roll(v, 23, 0) - pltpu.roll(v, 1, 0))[0:16]

    def plane_terms(x):
        p_s, p_d = along_z(0, x)
        u_s, _ = along_z(1, x)
        v_s, _ = along_z(2, x)
        _, w_d = along_z(3, x)
        return (
            smooth_y(p_s), spread_y(p_s), smooth_y(p_d),
            smooth_y(u_s), spread_y(v_s) + smooth_y(w_d),
        )

    terms = [plane_terms(0), plane_terms(1)]
    for x in range(8):
        terms.append(plane_terms(x + 2))
        before, here, after = terms[x : x + 3]
        gradient = (
            after[0] - before[0],
            before[1] + 2.0 * here[1] + after[1],
            before[2] + 2.0 * here[2] + after[2],
        )
        divergence = after[3] - before[3] + (before[4] + 2.0 * here[4] + after[4])
        rim[3, x] = divergence * (1.0 / 32.0)
        for k in range(3):
            rim[k, x] = gradient[k] * (1.0 / 32.0)

    delivered(contrib.at[0:38], RIM)
    received(max2.at[1:64], SPEED_CHIPS)
    largest = jnp.max(jnp.max(max2[...], axis=0), axis=1, keepdims=True)
    step = 0.5 / jnp.sqrt(1.0 + 0.05 * largest)
    step = jnp.broadcast_to(step, (16, 128))

    def advance(x):
        rows = slice(x * 16, x * 16 + 16)
        divergence = rim[3, x]
        pressure = fields[0, rows]
        fields[4, rows] = fields[4, rows] - step * pressure * divergence
        fields[0, rows] = pressure - step * divergence
        for k in range(3):
            fields[1 + k, rows] = fields[1 + k, rows] - step * rim[k, x]

    for x in range(8):
        advance(x)
    delivered(zsend, HALO_Z)
    delivered(pad.at[0:2, inner], HALO_X)
    delivered(pad.at[0, inner], HALO_Y)
    delivered(meta.at[0, 1:8], META_LINE)
    delivered(meta.at[1:16], META_PLANE)
    delivered(sendbuf.at[0:127], DELIVERY)
    delivered(max1.at[1:2], SPEED_CORE)
    delivered(max2.at[1:64], SPEED_CHIPS)


def on_device(old_state, remap_weights, new_owner, new_block):
    dma = pltpu.SemaphoreType.DMA
    hbm = pl.BlockSpec(memory_space=pltpu.HBM)
    vmem = pl.BlockSpec(memory_space=pltpu.VMEM)
    out = pl.pallas_call(
        kernel,
        out_shape=jax.ShapeDtypeStruct((16, 128, 128), F32),
        in_specs=[hbm, hbm, vmem],
        out_specs=vmem,
        scratch_shapes=[
            pltpu.VMEM((128, 512, 128), BF16),
            pltpu.VMEM((16, 8, 16, 128), F32),
            pltpu.VMEM((10, 18, 16, 128), F32),
            pltpu.VMEM((2, 16, 128), F32),
            pltpu.VMEM((2, 16, 128), F32),
            pltpu.VMEM((129, 16, 128), F32),
            pltpu.VMEM((128, 2, 16, 128), F32),
            pltpu.VMEM((128, 2, 16, 128), F32),
            pltpu.VMEM((16, 8, 2, 128), jnp.int32),
            pltpu.VMEM((2, 128, 128), jnp.int32),
            pltpu.VMEM((8, 128), jnp.int32),
            pltpu.SMEM((8, 128), jnp.int32),
            pltpu.VMEM((CHUNKS, 128, 128), BF16),
            pltpu.VMEM((16, 128, 128), BF16),
            pltpu.VMEM((4, 8, 16, 128), F32),
            pltpu.VMEM((2, 4, 16, 128), F32),
            pltpu.VMEM((2, 4, 8, 128), F32),
            pltpu.VMEM((2, 4, 8, 128), F32),
            pltpu.VMEM((2, 2, 4, 8, 128), F32),
            pltpu.VMEM((2, 16, 128), F32),
            pltpu.VMEM((2, 3, 3, 16, 128), F32),
            pltpu.VMEM((2, 8, 128), F32),
            pltpu.VMEM((64, 1, 128), F32),
            pltpu.SemaphoreType.REGULAR,
            dma((8,)), dma((1,)), dma((1,)), dma((9,)), dma((8 + CHUNKS,)),
        ],
        compiler_params=pltpu.CompilerParams(
            collective_id=0, has_side_effects=True, vmem_limit_bytes=52 * 2**20
        ),
        cost_estimate=pl.CostEstimate(flops=2 * 16 * 512 * 128 * 128, bytes_accessed=20 * 2**20, transcendentals=0),
    )(
        old_state,
        remap_weights.reshape(128, 512, 128),
        jnp.concatenate([new_owner.reshape(1, 128), new_block.reshape(1, 128)], axis=0),
    )
    return out.reshape(16, 8, 16, 128)


def solution(mesh):
    return jax.shard_map(
        on_device,
        mesh=mesh,
        in_specs=(
            P(None, "gx", "gy", "gz"),
            P(("gx", "gy", "gz"), None, None, None),
            P(("gx", "gy", "gz"), None),
            P(("gx", "gy", "gz")),
        ),
        out_specs=P(None, "gx", "gy", "gz"),
        check_vma=False,
    )
```
